32 devices in a mesh: ctx: 16 (over z, x, core), fsdp: 2 (over y).
Axes of the slice: x: 2, y: 2, z: 4, core: 2. Of those that a mesh axis runs over, the one named last changes fastest.
Arguments:
- streams: bfloat16 [3, 8192, 8192], P(None, ('ctx', 'fsdp')), may hold values from -6 to 6
- segments: int32 [8192], replicated, may hold values from 0 to 31, never falling along the last dimension, each value on 1 to 4096 neighbouring positions
- short_taps: float32 [3, 3, 8192], P(None, None, 'fsdp'), may hold values from -3 to 3
- decay_rates: float32 [512, 16], P('fsdp'), may hold values from 1.2207031e-05 to 0.1
- residues: float32 [512, 16], P('fsdp'), may hold values from -2 to 2
- skip_gain: float32 [8192], P('fsdp'), may hold values from -4 to 4
Outputs:
- output: bfloat16 [8192, 8192], P(('ctx', 'fsdp'))
The draws below stay inside these ranges and needn't reach their ends.
Inputs may be any that keep to these rules, and one draw needn't show every extreme that they name: `segments`: never falling along the window; every document has 1 to 4096 tokens and one has exactly 4096.
All inputs are finite; a program needn't handle non-finite values.
Results may differ from the reference program's by a relative error of at most 0.0064.
Values may be sent and summed in bfloat16 or wider, within the bound.
No kernel may reach another device: no remote copies, remote signals or barrier semaphores. Data moves between devices by JAX's collectives and lax.ppermute only.
A program may use at most 192 MiB of HBM per device.

```python
import math
import jax
import jax.numpy as jnp
import numpy as np
from jax import lax

D = 8192
GROUP = 16
MODES = 16
SHORT = 3
TOKENS = 8192
DOC_MAX = 4096
DOCS = 32
N_FSDP = 2


def draw_decay_rates(key, part):
    array_shape = (D // GROUP, MODES)
    return jnp.exp(jax.random.uniform(key, array_shape, jnp.float32, jnp.log(0.25 / DOC_MAX), jnp.log(0.1)))


def level_of(key, dims, cuts, least, largest):
    loudness = 1.0
    for position, shards_of in cuts:
        heights = jax.random.uniform(jax.random.fold_in(jax.random.fold_in(key, 6), position), (shards_of,), jnp.float32, least / len(cuts), largest / len(cuts))
        loudness = loudness * jnp.repeat(jnp.exp(heights), dims[position] // shards_of).reshape((-1,) + (1,) * (len(dims) - 1 - position))
    return loudness


def profile(number_of, total, reach, slope):
    portions = [(1 << 20) // math.isqrt(rank ** slope) + 1 for rank in range(2, number_of + 1)]
    surplus, given = total - reach - (number_of - 1), [1] * (number_of - 1)
    while surplus > 0:
        free = [i for i in range(number_of - 1) if given[i] < reach]
        whole, budget = sum([portions[i] for i in free]), surplus
        for i in free:
            more = min(reach - given[i], max(1, budget * portions[i] // whole), surplus)
            given[i] = given[i] + more
            surplus = surplus - more
    return np.array([reach] + given)


def uneven(key, count, total, most, skew):
    if count == 2:
        one = jax.random.randint(key, (), max(1, total - most), min(most, total - 1) + 1)
        return jnp.stack([one, total - one])
    lengths = jnp.asarray(profile(count, total, most, skew), jnp.int32)
    couples = (count - 1) // 2
    donor, taker = lengths[1:1 + 2 * couples:2], lengths[2:2 + 2 * couples:2]
    room = jnp.minimum(donor - 1, most - taker)
    moved = jax.random.randint(jax.random.fold_in(key, 1), (couples,), 0, 1 << 20) % (room + 1)
    lengths = lengths.at[1:1 + 2 * couples:2].set(donor - moved).at[2:2 + 2 * couples:2].set(taker + moved)
    return lengths[jax.random.permutation(jax.random.fold_in(key, 2), count)]


def centred(rng, shape, spread, bound, cuts=(), kind=jnp.bfloat16):
    loudness = level_of(rng, shape, cuts, -0.22, 0.18) if cuts else 1.0
    values = jax.random.normal(rng, shape, jnp.float32) * spread * loudness
    return jnp.minimum(jnp.maximum(values, -bound), bound).astype(kind)


def setup_inputs(seed: int = 0) -> dict:
    key_of = jax.random.split(jax.random.key(seed), 7)
    streams = centred(key_of[0], (3, TOKENS, D), 1.0, 6.0, ((1, 32),))
    segments = jnp.searchsorted(jnp.cumsum(uneven(key_of[1], DOCS, TOKENS, DOC_MAX, 2)), jnp.arange(TOKENS), side="right").astype(jnp.int32)
    short_taps = centred(key_of[2], (3, SHORT, D), 0.6, 3.0, ((2, 2),), jnp.float32)
    decay_rates = draw_decay_rates(jax.random.fold_in(key_of[6], 71), 0)
    residues = centred(key_of[4], (D // GROUP, MODES), 0.35, 2.0, ((0, 2),), jnp.float32)
    skip_gain = centred(key_of[5], (D,), 1.0, 4.0, ((0, 2),), jnp.float32)
    return {"streams": streams, "segments": segments, "short_taps": short_taps, "decay_rates": decay_rates, "residues": residues, "skip_gain": skip_gain}


def featured_stream(stream, stream_taps, earlier_marks):
    values = stream.astype(jnp.float32)
    summed = values * stream_taps[0]
    for offset in range(1, SHORT):
        shifted = jnp.concatenate([jnp.zeros((offset, values.shape[1]), jnp.float32), values[:-offset]], axis=0)
        summed = summed + jnp.where(earlier_marks[offset - 1][:, None], shifted, 0.0) * stream_taps[offset]
    return summed

def reference(streams, segments, short_taps, decay_rates, residues, skip_gain):
    block_width = D // N_FSDP
    block_groups = block_width // GROUP
    earlier_marks = [jnp.concatenate([jnp.full((offset,), -1, jnp.int32), segments[:-offset]]) == segments for offset in range(1, SHORT)]
    continues = earlier_marks[0].astype(jnp.float32)

    def one_block(block_index):
        first_col = block_index * block_width
        columns = lax.dynamic_slice_in_dim(streams, first_col, block_width, 2)
        block_taps = lax.dynamic_slice_in_dim(short_taps, first_col, block_width, 2)
        first_group = block_index * block_groups
        block_rates = lax.dynamic_slice_in_dim(decay_rates, first_group, block_groups, 0)
        block_residues = lax.dynamic_slice_in_dim(residues, first_group, block_groups, 0)
        block_skip = lax.dynamic_slice_in_dim(skip_gain, first_col, block_width, 0)
        queries = featured_stream(columns[0], block_taps[0], earlier_marks).astype(jnp.bfloat16)
        gated_prod = (featured_stream(columns[1], block_taps[1], earlier_marks) * featured_stream(columns[2], block_taps[2], earlier_marks)).astype(jnp.bfloat16)
        queries, gated_prod = lax.optimization_barrier((queries, gated_prod))
        decays = jnp.repeat(jnp.exp(-block_rates), GROUP, axis=0).T
        mode_gain = jnp.repeat(block_residues * jnp.sqrt(-jnp.expm1(-2.0 * block_rates)), GROUP, axis=0).T

        def advance(carried, inputs):
            current, keep_flag = inputs
            carried = keep_flag * decays * carried + current[None, :]
            return (carried, lax.optimization_barrier(jnp.sum(mode_gain * carried, axis=0)))
        start_state = jnp.zeros((MODES, block_width), jnp.float32)
        gated_values = gated_prod.astype(jnp.float32)
        unused, filtered = lax.scan(advance, start_state, (gated_values, continues))
        mixed_out = (filtered + block_skip * gated_values).astype(jnp.bfloat16)
        mixed_out = lax.optimization_barrier(mixed_out)
        return (queries.astype(jnp.float32) * mixed_out.astype(jnp.float32)).astype(jnp.bfloat16)
    blocks = lax.map(one_block, jnp.arange(N_FSDP, dtype=jnp.int32))
    return jnp.transpose(blocks, (1, 0, 2)).reshape(TOKENS, D)
```

```python
import functools

import jax
import jax.numpy as jnp
from jax import lax
from jax.experimental import pallas as pl
from jax.experimental.pallas import tpu as pltpu
from jax.sharding import PartitionSpec as P

GROUP = 16
MODES = 16
SHORT = 3
LANES = 128
TILE_GROUPS = LANES // GROUP
F32 = jnp.float32
BF16 = jnp.bfloat16
VMEM_BYTES = 48 * 1024 * 1024


def mark_rows(marks_ref, before_ref, block):
    marks = marks_ref[0].astype(F32)
    before = jnp.where(block > 0, before_ref[0], -1).astype(F32)
    lane = lax.broadcasted_iota(jnp.int32, marks.shape, 1)
    rows = [marks]
    for offset in range(1, SHORT):
        rows.append(
            jnp.where(
                lane < offset, pltpu.roll(before, offset, 1), pltpu.roll(marks, offset, 1)
            )
        )
    return rows


def as_column(row):
    return jnp.transpose(jnp.broadcast_to(row, (LANES, row.shape[1])))


def featured(x_ref, stream, lanes, halo, taps, agree_refs, row_block):
    rows = x_ref.shape[1]
    for start in range(0, rows, row_block):
        if start == 0:
            here = x_ref[stream, 0:row_block, lanes].astype(F32)
            sub = lax.broadcasted_iota(jnp.int32, (8, LANES), 0)
            ahead = jnp.where(sub == 6, halo[0:1], jnp.where(sub == 7, halo[1:2], 0.0))
        else:
            both = x_ref[stream, start - 16 : start + row_block, lanes].astype(F32)
            here, ahead = both[16:], both[8:16]
        joined = jnp.concatenate([ahead, here], axis=0)
        span = slice(start, start + row_block)
        summed = here * taps[0:1]
        for offset in range(1, SHORT):
            shifted = pltpu.roll(joined, offset, 0)[8:]
            summed = summed + shifted * agree_refs[offset - 1, span, :] * taps[offset : offset + 1]
        yield span, summed


def set_agree(agree_ref, rows):
    mark = as_column(rows[0])
    for offset in range(1, SHORT):
        agree_ref[offset - 1] = jnp.where(mark == as_column(rows[offset]), 1.0, 0.0)


def state_kernel(
    block_ref, x_ref, halo_ref, pack_ref, marks_ref, before_ref,
    gated_ref, state_ref, rates_ref, agree_ref, last_ref,
):
    tokens = x_ref.shape[1]

    @pl.when(pl.program_id(0) == 0)
    def _():
        rows = mark_rows(marks_ref, before_ref, block_ref[0])
        set_agree(agree_ref, rows)
        last = rows[0][:, tokens - 1 :]
        last_ref[...] = jnp.broadcast_to(jnp.where(rows[0] == last, 1.0, 0.0), last_ref.shape)

    @pl.loop(0, x_ref.shape[2] // LANES)
    def _(tile):
        lanes = pl.ds(pl.multiple_of(tile * LANES, LANES), LANES)
        key_halo = halo_ref[1, :, lanes].astype(F32)
        value_halo = halo_ref[2, :, lanes].astype(F32)
        keys = featured(x_ref, 0, lanes, key_halo, pack_ref[3:6, lanes], agree_ref, 64)
        values = featured(x_ref, 1, lanes, value_halo, pack_ref[6:9, lanes], agree_ref, 64)
        for (span, key), (_, value) in zip(keys, values):
            gated_ref[span, lanes] = (key * value).astype(BF16)
        rate_row = pack_ref[10:11, lanes]
        rate = as_column(rate_row)
        rate = jnp.concatenate([rate] * (tokens // LANES), axis=1)
        left = (tokens - 1) - lax.broadcasted_iota(jnp.int32, rate.shape, 1)
        falling = jnp.exp(-rate * left.astype(F32)) * last_ref[0:1, :]
        full = jnp.dot(
            falling.astype(BF16), gated_ref[:, lanes], preferred_element_type=F32
        )
        own = lax.broadcasted_iota(jnp.int32, (MODES, LANES), 1) // GROUP
        state = jnp.zeros((MODES, LANES), F32)
        for group in range(TILE_GROUPS):
            state = jnp.where(own == group, full[group * MODES : (group + 1) * MODES], state)
        state_ref[:, lanes] = state.astype(BF16)
        mode = lax.broadcasted_iota(jnp.int32, (MODES, LANES), 0)
        rates_ref[:, lanes] = jnp.take_along_axis(
            jnp.broadcast_to(rate_row, (MODES, LANES)), own * GROUP + mode, axis=1
        )


def local_kernel(
    block_ref, gated_ref, pack_ref, marks_ref, before_ref, *rest
):
    out_ref, causal_ref = rest[-2:]
    tokens = gated_ref.shape[0]

    @pl.when(pl.program_id(0) == 0)
    def _():
        row = marks_ref[0].astype(F32)
        column = as_column(row)
        column = jnp.concatenate([column] * (tokens // LANES), axis=1)
        later = lax.broadcasted_iota(jnp.int32, column.shape, 0)
        earlier = lax.broadcasted_iota(jnp.int32, column.shape, 1)
        causal_ref[...] = jnp.where((column == row) & (later >= earlier), 1.0, 0.0).astype(BF16)

    @pl.loop(0, gated_ref.shape[1] // LANES)
    def _(tile):
        lanes = pl.ds(pl.multiple_of(tile * LANES, LANES), LANES)
        rate = as_column(pack_ref[10:11, lanes])
        gain = as_column(pack_ref[11:12, lanes])
        rate = jnp.concatenate([rate] * (tokens // LANES), axis=1)
        gain = jnp.concatenate([gain] * (tokens // LANES), axis=1)
        left = (tokens - 1) - lax.broadcasted_iota(jnp.int32, rate.shape, 1)
        terms = gain * jnp.exp(-rate * left.astype(F32))
        taps = jnp.sum(terms.reshape(TILE_GROUPS, MODES, tokens), axis=1)
        own = lax.broadcasted_iota(jnp.int32, (1, LANES), 1) // GROUP
        half = tokens // 2
        upper = jnp.zeros((half, LANES), F32)
        lower = jnp.zeros((half, LANES), F32)
        for group in range(TILE_GROUPS):
            base = pltpu.roll(
                jnp.broadcast_to(taps[group : group + 1], (8, tokens)),
                1, 1, stride=1, stride_axis=0,
            )
            pieces = [base] + [pltpu.roll(base, 8 * i, 1) for i in range(1, half // 8)]
            top = jnp.concatenate(pieces, axis=0).astype(BF16)
            bottom = jnp.concatenate([top[:, half:], top[:, :half]], axis=1)
            top = top[:, :half] * causal_ref[:half, :half]
            bottom = bottom * causal_ref[half:, :]
            upper = jnp.where(
                own == group,
                jnp.dot(top, gated_ref[:half, lanes], preferred_element_type=F32),
                upper,
            )
            lower = jnp.where(
                own == group,
                jnp.dot(bottom, gated_ref[:, lanes], preferred_element_type=F32),
                lower,
            )
        skip = pack_ref[9:10, lanes]
        out_ref[:half, lanes] = upper + skip * gated_ref[:half, lanes].astype(F32)
        out_ref[half:, lanes] = lower + skip * gated_ref[half:, lanes].astype(F32)


def output_kernel(
    block_ref, x_ref, halo_ref, pack_ref, marks_ref, before_ref, local_ref, carry_ref,
    out_ref, agree_ref, follow_ref,
):
    tokens = x_ref.shape[1]

    @pl.when(pl.program_id(0) == 0)
    def _():
        rows = mark_rows(marks_ref, before_ref, block_ref[0])
        set_agree(agree_ref, rows)
        follow_ref[...] = as_column(jnp.where(rows[0] == rows[1][:, 0:1], 1.0, 0.0))

    @pl.loop(0, x_ref.shape[2] // LANES)
    def _(tile):
        lanes = pl.ds(pl.multiple_of(tile * LANES, LANES), LANES)
        own = lax.broadcasted_iota(jnp.int32, (MODES, LANES), 1) // GROUP
        mode = lax.broadcasted_iota(jnp.int32, (MODES, LANES), 0)
        gain = jnp.take_along_axis(
            jnp.broadcast_to(pack_ref[11:12, lanes], (MODES, LANES)), own * GROUP + mode, axis=1
        )
        scaled = gain * carry_ref[:, lanes].astype(F32)
        spread = jnp.concatenate(
            [jnp.where(own == group, scaled, 0.0) for group in range(TILE_GROUPS)], axis=0
        ).astype(BF16)
        age = lax.broadcasted_iota(jnp.int32, (tokens, LANES), 0) + 1
        rising = jnp.exp(-pack_ref[10:11, lanes] * age.astype(F32)) * follow_ref[...]
        carried = jnp.dot(rising.astype(BF16), spread, preferred_element_type=F32)
        halo = halo_ref[0, :, lanes].astype(F32)
        for span, query in featured(x_ref, 0, lanes, halo, pack_ref[0:3, lanes], agree_ref, 64):
            mixed = (local_ref[span, lanes] + carried[span]).astype(BF16)
            out_ref[span, lanes] = (
                query.astype(BF16).astype(F32) * mixed.astype(F32)
            ).astype(BF16)


def cost(flops, size, exps):
    return pl.CostEstimate(flops=flops, bytes_accessed=size, transcendentals=exps)


def mark_specs(tokens):
    return [
        pl.BlockSpec((1, 1, tokens), lambda i, b: (b[0], 0, 0)),
        pl.BlockSpec((1, 1, tokens), lambda i, b: (jnp.maximum(b[0] - 1, 0), 0, 0)),
    ]


def block_states(block, streams, halo, pack, marks, width):
    _, tokens, channels = streams.shape
    return pl.pallas_call(
        state_kernel,
        grid_spec=pltpu.PrefetchScalarGridSpec(
            num_scalar_prefetch=1,
            grid=(channels // width,),
            in_specs=[
                pl.BlockSpec((pl.Element(2), pl.Element(tokens), pl.Element(width)),
                             lambda i, b: (1, 0, i * width)),
                pl.BlockSpec((3, SHORT - 1, width), lambda i, b: (0, 0, i)),
                pl.BlockSpec((pack.shape[0], width), lambda i, b: (0, i)),
                *mark_specs(tokens),
            ],
            out_specs=[
                pl.BlockSpec((tokens, width), lambda i, b: (0, i)),
                pl.BlockSpec((MODES, width), lambda i, b: (0, i)),
                pl.BlockSpec((MODES, width), lambda i, b: (0, i)),
            ],
            scratch_shapes=[
                pltpu.VMEM((SHORT - 1, tokens, LANES), F32),
                pltpu.VMEM((8, tokens), F32),
            ],
        ),
        out_shape=[
            jax.ShapeDtypeStruct((tokens, channels), BF16),
            jax.ShapeDtypeStruct((MODES, channels), BF16),
            jax.ShapeDtypeStruct((MODES, channels), F32),
        ],
        compiler_params=pltpu.CompilerParams(vmem_limit_bytes=VMEM_BYTES),
        cost_estimate=cost(20 * tokens * channels, 6 * tokens * channels, tokens * channels),
        name="block_states",
    )(block, streams, halo, pack, marks, marks)


def block_local(block, gated, pack, marks, held, first, count, width):
    tokens, channels = gated.shape
    at = first // width
    return pl.pallas_call(
        local_kernel,
        grid_spec=pltpu.PrefetchScalarGridSpec(
            num_scalar_prefetch=1,
            grid=(count // width,),
            in_specs=[
                pl.BlockSpec((tokens, width), lambda i, b: (0, i + at)),
                pl.BlockSpec((pack.shape[0], width), lambda i, b: (0, i + at)),
                *mark_specs(tokens),
                *[pl.BlockSpec(memory_space=pl.ANY) for _ in held],
            ],
            out_specs=pl.BlockSpec((tokens, width), lambda i, b: (0, i + at)),
            scratch_shapes=[pltpu.VMEM((tokens, tokens), BF16)],
        ),
        out_shape=jax.ShapeDtypeStruct((tokens, channels), F32),
        input_output_aliases={5: 0} if held else {},
        compiler_params=pltpu.CompilerParams(vmem_limit_bytes=VMEM_BYTES),
        cost_estimate=cost(
            2 * tokens * tokens * count * TILE_GROUPS, 6 * tokens * count, tokens * count
        ),
        name="block_local",
    )(block, gated, pack, marks, marks, *held)


def block_output(block, streams, halo, pack, marks, held, carry, width):
    _, tokens, channels = streams.shape
    return pl.pallas_call(
        output_kernel,
        grid_spec=pltpu.PrefetchScalarGridSpec(
            num_scalar_prefetch=1,
            grid=(channels // width,),
            in_specs=[
                pl.BlockSpec((1, tokens, width), lambda i, b: (0, 0, i)),
                pl.BlockSpec((3, SHORT - 1, width), lambda i, b: (0, 0, i)),
                pl.BlockSpec((pack.shape[0], width), lambda i, b: (0, i)),
                *mark_specs(tokens),
                pl.BlockSpec((tokens, width), lambda i, b: (0, i)),
                pl.BlockSpec((MODES, width), lambda i, b: (0, i)),
            ],
            out_specs=pl.BlockSpec((tokens, width), lambda i, b: (0, i)),
            scratch_shapes=[
                pltpu.VMEM((SHORT - 1, tokens, LANES), F32),
                pltpu.VMEM((tokens, LANES), F32),
            ],
        ),
        out_shape=jax.ShapeDtypeStruct((tokens, channels), BF16),
        compiler_params=pltpu.CompilerParams(vmem_limit_bytes=VMEM_BYTES),
        cost_estimate=cost(20 * tokens * channels, 8 * tokens * channels, tokens * channels),
        name="block_output",
    )(block, streams, halo, pack, marks, marks, held, carry)


SPAN = 8


def shifted_2(block, axis, distance):
    devices = range(lax.axis_size(axis))
    route = [(i - distance, i) for i in devices if i - distance in devices]
    return lax.ppermute(block, axis, route)


def contract(pattern, left_side, right_side):
    return jnp.einsum(pattern, left_side, right_side, precision=lax.Precision.HIGHEST)


def featurize(block_rows, before_rows, tap_rows, row_marks, before_marks):
    margin = before_rows.shape[1]
    row_count = block_rows.shape[1]
    joined = jnp.concatenate([before_rows, block_rows], axis=1)
    all_marks = jnp.concatenate([before_marks, row_marks])
    summed = block_rows.astype(jnp.float32) * tap_rows[:, 0][:, None, :]
    for offset in range(1, margin + 1):
        shifted = joined[:, margin - offset : margin - offset + row_count].astype(jnp.float32)
        agreeing = all_marks[margin - offset : margin - offset + row_count] == row_marks
        summed = (
            summed
            + jnp.where(agreeing[None, :, None], shifted, 0.0) * tap_rows[:, offset][:, None, :]
        )
    queries = summed[0].astype(jnp.bfloat16)
    gated_prod = (summed[1] * summed[2]).astype(jnp.bfloat16)
    return lax.optimization_barrier((queries, gated_prod))


def tile_filter(gated_prod, tile_marks, decay_rates, mode_gain, rising):
    tile_rows, channels = gated_prod.shape
    groups = channels // GROUP
    block_len = min(128, tile_rows)
    offsets = jnp.arange(block_len, dtype=jnp.float32)
    forward = mode_gain[:, :, None] * jnp.exp(-decay_rates[:, :, None] * offsets)
    backward = jnp.exp(decay_rates[:, :, None] * offsets)
    causal = (offsets[:, None] >= offsets[None, :]).astype(jnp.float32)
    kernel = contract("gmt,gms->gts", forward, backward) * causal
    mode_rates = decay_rates.T[:, :, None]
    closing = jnp.exp(-mode_rates * (block_len - 1.0 - offsets))
    through = jnp.exp(-mode_rates * block_len)
    head_rising = rising[:, :, :block_len]
    values = gated_prod.astype(jnp.float32).reshape(tile_rows, groups, GROUP)
    carried = jnp.zeros((MODES, groups, GROUP), jnp.float32)
    last_seen = jnp.int32(-1)
    pieces = []
    for number in range(tile_rows // block_len):
        block_vals = values[number * block_len : (number + 1) * block_len]
        block_marks = tile_marks[number * block_len : (number + 1) * block_len]
        agreeing = (block_marks[:, None] == block_marks[None, :]).astype(jnp.float32)
        inside = contract("gts,sgc->tgc", kernel * agreeing, block_vals)
        follow = (block_marks == last_seen).astype(jnp.float32)
        inside = inside + follow[:, None, None] * contract("mgt,mgc->tgc", head_rising, carried)
        ending = (block_marks == block_marks[block_len - 1]).astype(jnp.float32)
        fresh_state = contract("mgs,sgc->mgc", closing * ending, block_vals)
        passing = (block_marks[block_len - 1] == last_seen).astype(jnp.float32)
        carried = fresh_state + passing * through * carried
        last_seen = block_marks[block_len - 1]
        pieces.append(inside)
    return (jnp.concatenate(pieces, axis=0), carried)


def narrow_local(streams, segments, short_taps, decay_rates, residues, skip_gain):
    fsdp_count = lax.axis_size("fsdp")
    ctx_count = lax.axis_size("ctx")
    tile_index = lax.axis_index("ctx")
    own_rows = streams.shape[1]
    tile_rows = own_rows * fsdp_count
    margin = SHORT - 1
    padded_marks = jnp.concatenate([jnp.full((margin,), -1, jnp.int32), segments])
    tile_start = tile_index * tile_rows
    tile_marks = lax.dynamic_slice_in_dim(segments, tile_start, tile_rows)
    local_streams = lax.all_to_all(streams, "fsdp", split_axis=2, concat_axis=1, tiled=True)
    before_rows = shifted_2(local_streams[:, tile_rows - margin :, :], "ctx", 1)
    before_marks = lax.dynamic_slice_in_dim(padded_marks, tile_start, margin)
    queries, gated_prod = featurize(
        local_streams, before_rows, short_taps, tile_marks, before_marks
    )
    channels = gated_prod.shape[1]
    groups = channels // GROUP
    mode_gain = residues * jnp.sqrt(-jnp.expm1(-2.0 * decay_rates))
    positions = jnp.arange(tile_rows, dtype=jnp.float32)
    mode_rates = decay_rates.T[:, :, None]
    rising = mode_gain.T[:, :, None] * jnp.exp(-mode_rates * (positions + 1.0))
    local_part, end_state = tile_filter(gated_prod, tile_marks, decay_rates, mode_gain, rising)
    first_mark = tile_marks[0]
    falling = jnp.exp(-mode_rates * (tile_rows - 1.0 - positions))

    def source_state(operand):
        source_vals, source_marks = operand
        chosen = (source_marks == first_mark).astype(jnp.float32)
        return contract(
            "mgs,sgc->mgc",
            falling * chosen,
            source_vals.astype(jnp.float32).reshape(tile_rows, groups, GROUP),
        )

    def empty_state(operand):
        return jnp.zeros((MODES, groups, GROUP), jnp.float32)

    prior_state = jnp.zeros((MODES, groups, GROUP), jnp.float32)
    for distance in range(1, min(SPAN, ctx_count - 1) + 1):
        source_tile = shifted_2(gated_prod, "ctx", distance)
        source_index = tile_index - distance
        source_marks = lax.dynamic_slice_in_dim(
            segments, jnp.maximum(source_index, 0) * tile_rows, tile_rows
        )
        paired = (source_index >= 0) & (source_marks[tile_rows - 1] == first_mark)
        received = lax.cond(paired, source_state, empty_state, (source_tile, source_marks))
        prior_state = prior_state + jnp.exp(-mode_rates * ((distance - 1) * tile_rows)) * received
    prior_mark = first_mark.astype(jnp.float32)
    follow_tile = (tile_marks.astype(jnp.float32) == prior_mark).astype(jnp.float32)
    filtered = local_part + follow_tile[:, None, None] * contract(
        "mgt,mgc->tgc", rising, prior_state
    )
    mixed_out = (
        filtered.reshape(tile_rows, channels) + skip_gain * gated_prod.astype(jnp.float32)
    ).astype(jnp.bfloat16)
    mixed_out = lax.optimization_barrier(mixed_out)
    payload = (queries.astype(jnp.float32) * mixed_out.astype(jnp.float32)).astype(jnp.bfloat16)
    returned = lax.all_to_all(payload, "fsdp", split_axis=0, concat_axis=1, tiled=True)
    return returned


def half_of(array, which):
    size = array.shape[1] // 2
    return lax.dynamic_slice_in_dim(array, which * size, size, axis=1)


def swap(array, distance, devices):
    route = [(i, i ^ distance) for i in range(devices)]
    return lax.ppermute(array.astype(BF16), ("ctx", "fsdp"), route).astype(F32)


def ordered(which, mine, other):
    return jnp.where(which == 0, mine, other), jnp.where(which == 0, other, mine)


def joined_halves(which, mine, other):
    return jnp.concatenate(ordered(which, mine, other), axis=1)


def carry_in(state, rates, marks, block, devices, tokens):
    ends = marks[:, 0, tokens - 1]
    places = jnp.arange(devices)

    def end_of(index):
        return jnp.sum(jnp.where(places == index, ends, 0))

    def passes(earlier, later):
        return (end_of(earlier) == end_of(later)).astype(F32)

    def decay(rate, blocks):
        return jnp.exp(-rate * (jnp.maximum(blocks, 0) * tokens).astype(F32))

    one = jnp.int32(1)
    low, high = block & 1, (block >> 1) & 1
    pair, quad = block & ~1, block & ~3
    mine = half_of(state, low).astype(F32)
    other = swap(half_of(state, 1 - low), 1, devices)
    first, second = ordered(low, mine, other)
    rate = half_of(rates, low)
    pair_end = second + passes(pair, pair + 1) * decay(rate, one) * first
    mine = half_of(pair_end, high)
    other = swap(half_of(pair_end, 1 - high), 2, devices)
    lower, upper = ordered(high, mine, other)
    narrow = half_of(rate, high)
    total = upper + passes(quad + 1, quad + 3) * decay(narrow, 2 * one) * lower
    carry = jnp.zeros_like(total)
    size = 4
    while size < devices:
        other = swap(total, size, devices)
        start = (block // (2 * size)) * (2 * size)
        upside = (block // size) & 1
        middle = start + size - 1
        weight = upside.astype(F32) * passes(middle, quad - 1)
        carry = carry + weight * decay(narrow, quad - 1 - middle) * other
        if 2 * size < devices:
            before, after = ordered(upside, total, other)
            total = after + passes(middle, middle + size) * decay(narrow, size * one) * before
        size *= 2
    ahead = lower + passes(quad - 1, quad + 1) * decay(narrow, 2 * one) * carry
    keep, send = ordered(high, carry, ahead)
    carry = joined_halves(high, keep, swap(send, 2, devices))
    ahead = first + passes(pair - 1, pair) * decay(rate, one) * carry
    keep, send = ordered(low, carry, ahead)
    other = swap(send, 1, devices)
    return joined_halves(low, keep, other).astype(BF16)


def gather_weights(pack, fsdp_count, index):
    if fsdp_count != 2:
        return lax.all_gather(pack, "fsdp", axis=1, tiled=True)
    other = lax.ppermute(pack, "fsdp", [(0, 1), (1, 0)])
    return joined_halves(index, pack, other)


def local(streams, segments, short_taps, decay_rates, residues, skip_gain):
    fsdp_count, ctx_count = lax.axis_size("fsdp"), lax.axis_size("ctx")
    devices = fsdp_count * ctx_count
    _, tokens, channels = streams.shape
    if tokens % LANES:
        return narrow_local(streams, segments, short_taps, decay_rates, residues, skip_gain)
    fsdp_index = lax.axis_index("fsdp")
    block = lax.axis_index("ctx") * fsdp_count + fsdp_index
    block_ref = block.astype(jnp.int32).reshape(1)
    owned = short_taps.shape[2]
    mode_gain = residues * jnp.sqrt(-jnp.expm1(-2.0 * decay_rates))
    pack = jnp.concatenate(
        [
            short_taps.reshape(3 * SHORT, owned),
            skip_gain.reshape(1, owned),
            decay_rates.reshape(1, owned),
            mode_gain.reshape(1, owned),
        ],
        axis=0,
    )
    pack = gather_weights(pack, fsdp_count, fsdp_index)
    halo = lax.ppermute(
        streams[:, tokens - (SHORT - 1) :, :], ("ctx", "fsdp"),
        [(i, i + 1) for i in range(devices - 1)],
    )
    marks = segments.reshape(devices, 1, tokens)
    gated, state, rates = block_states(block_ref, streams, halo, pack, marks, 1024)
    held = []
    parts = 4
    span = channels // parts
    for part in range(parts):
        held = [block_local(block_ref, gated, pack, marks, held, part * span, span, 1024)]
    carry = carry_in(state, rates, marks, block, devices, tokens)
    return block_output(block_ref, streams, halo, pack, marks, held[0], carry, 1024)


def solution(mesh):
    placed = (
        P(None, ("ctx", "fsdp"), None),
        P(),
        P(None, None, "fsdp"),
        P("fsdp", None),
        P("fsdp", None),
        P("fsdp"),
    )
    return jax.shard_map(
        local, mesh=mesh, in_specs=placed, out_specs=P(("ctx", "fsdp"), None), check_vma=False
    )
```

```python
import jax
import jax.numpy as jnp
from jax import lax
from jax.experimental import pallas as pl
from jax.experimental.pallas import tpu as pltpu
from jax.sharding import PartitionSpec as P

GROUP = 16
MODES = 16
SHORT = 3
LANES = 128
PART = 128
PARTS = 2
WIDE = 256
COPIES = 4
TILES = 4
TILE_GROUPS = LANES // GROUP
ROWS = 64
LOG2E = 1.4426950408889634
F32 = jnp.float32
BF16 = jnp.bfloat16
VMEM = pl.BlockSpec(memory_space=pltpu.VMEM)
SMEM = pl.BlockSpec(memory_space=pltpu.SMEM)
HBM = pl.BlockSpec(memory_space=pltpu.HBM)
ANY = pl.BlockSpec(memory_space=pl.ANY)
SKIP, RATE, GAIN, PACKED = 9, 10, 11, 16
OWN, OTHER, LOW, HIGH, UPSIDES = 0, 1, 2, 3, 4
PAIR_PASS, QUAD_PASS, QUAD_FROM, PAIR_FROM, ROUNDS = 0, 1, 2, 3, 4


def iota(shape, axis):
    return lax.broadcasted_iota(jnp.int32, shape, axis)


def flag(condition):
    return jnp.where(condition, 1.0, 0.0)


def as_column(row):
    return jnp.transpose(jnp.broadcast_to(row, (LANES, row.shape[1])))


def lanes_at(start, size=LANES):
    return pl.ds(pl.multiple_of(start, LANES), size)


def weave(*lists):
    order = sorted(
        ((i + 0.5) / len(jobs), n, i) for n, jobs in enumerate(lists) for i in range(len(jobs))
    )
    for _, n, i in order:
        lists[n][i]()


def featured(x_ref, lanes, taps, agree_ref, start, halo):
    if start == 0:
        here = x_ref[0:ROWS, lanes].astype(F32)
        sub = iota((8, LANES), 0)
        ahead = jnp.where(sub == 6, halo[0:1], jnp.where(sub == 7, halo[1:2], 0.0))
    else:
        both = x_ref[start - 16 : start + ROWS, lanes].astype(F32)
        here, ahead = both[16:], both[8:16]
    joined = jnp.concatenate([ahead, here], axis=0)
    summed = here * taps[0:1]
    for offset in range(1, SHORT):
        shifted = pltpu.roll(joined, offset, 0)[8:]
        agree = agree_ref[offset - 1, start : start + ROWS, :]
        summed = summed + shifted * agree * taps[offset : offset + 1]
    return summed


def spread(state):
    own = iota(state.shape, 1) // GROUP
    return jnp.concatenate(
        [jnp.where(own == group, state, 0.0) for group in range(TILE_GROUPS)], axis=0
    ).astype(BF16)


def diagonal(full):
    own = iota((MODES, LANES), 1) // GROUP
    state = full[:MODES]
    for group in range(1, TILE_GROUPS):
        state = jnp.where(own == group, full[group * MODES : (group + 1) * MODES], state)
    return state


def pack_weights(short_ref, skip_ref, rates_ref, residues_ref, pack_ref):
    for stream in range(3):
        pack_ref[stream * SHORT : (stream + 1) * SHORT, :] = short_ref[stream]
    pack_ref[SKIP : SKIP + 1, :] = skip_ref[...]
    pack_ref[GAIN + 1 :, :] = jnp.zeros((PACKED - GAIN - 1, pack_ref.shape[1]), F32)
    shape = (MODES, LANES)
    own = iota(shape, 1) % MODES == iota(shape, 0)

    def tile(number, carried):
        at = lanes_at(number * LANES)
        first = number * TILE_GROUPS
        source = lanes_at(first // LANES * LANES)
        index = first % LANES + iota(shape, 1) // MODES
        rate = jnp.take_along_axis(rates_ref[:, source], index, axis=1)
        factor = jnp.take_along_axis(residues_ref[:, source], index, axis=1)
        rate = jnp.sum(jnp.where(own, rate, 0.0), axis=0, keepdims=True)
        factor = jnp.sum(jnp.where(own, factor, 0.0), axis=0, keepdims=True)
        half = jnp.tanh(rate)
        pack_ref[RATE : RATE + 1, at] = rate
        pack_ref[GAIN : GAIN + 1, at] = factor * jnp.sqrt(2.0 * half / (1.0 + half))
        return carried

    lax.fori_loop(0, pack_ref.shape[1] // LANES, tile, 0, unroll=4)


def place_kernel(
    spots_ref, marks_ref, short_ref, skip_ref, rates_ref, residues_ref, x_ref,
    place_ref, weights_ref, agree_ref, causal_ref, follow_ref, enter_ref, chosen_ref, pack_ref, tail_ref,
    ends_ref, sem, *, devices, tokens, fsdp_count,
):
    owned = pack_ref.shape[1]
    lines = tokens // LANES
    tail = pltpu.make_async_copy(x_ref.at[:, pl.ds(tokens - 16, 16), :], ends_ref, sem)
    tail.start()
    pack_weights(short_ref, skip_ref, rates_ref, residues_ref, pack_ref)
    fsdp_index = lax.axis_index("fsdp")
    block = lax.axis_index("ctx") * fsdp_count + fsdp_index
    place_ref[OWN] = fsdp_index * owned
    place_ref[OTHER] = (1 - fsdp_index) * owned
    place_ref[LOW] = lax.rem(block, 2)
    place_ref[HIGH] = lax.rem(lax.div(block, 2), 2)
    pair = block - lax.rem(block, 2)
    quad = block - lax.rem(block, 4)

    def end_of(index):
        return spots_ref[jnp.maximum(index, 0) * lines + lines - 1, LANES - 1]

    def passes(earlier, later):
        return jnp.where(end_of(earlier) == end_of(later), 1.0, 0.0)

    weights_ref[PAIR_PASS] = passes(pair, pair + 1)
    weights_ref[QUAD_PASS] = passes(quad + 1, quad + 3)
    weights_ref[QUAD_FROM] = passes(quad - 1, quad + 1)
    weights_ref[PAIR_FROM] = passes(pair - 1, pair)
    size, number = 4, 0
    while size < devices:
        start = block - lax.rem(block, 2 * size)
        upside = lax.rem(lax.div(block, size), 2)
        middle = start + size - 1
        place_ref[UPSIDES + number] = upside
        at = ROUNDS + 3 * number
        weights_ref[at] = jnp.where(upside == 1, passes(middle, quad - 1), 0.0)
        weights_ref[at + 1] = (jnp.maximum(quad - 1 - middle, 0) * tokens).astype(F32)
        weights_ref[at + 2] = passes(middle, middle + size)
        size, number = 2 * size, number + 1

    def marks_of(index):
        return jnp.concatenate(
            [marks_ref[pl.ds(index * lines + line, 1), :] for line in range(lines)], axis=1
        ).astype(F32)

    marks = marks_of(block)
    before = jnp.where(block > 0, marks_of(jnp.maximum(block - 1, 0)), -1.0)
    column = as_column(marks)
    lane = iota(marks.shape, 1)
    for offset in range(1, SHORT):
        row = jnp.where(lane < offset, pltpu.roll(before, offset, 1), pltpu.roll(marks, offset, 1))
        agree_ref[offset - 1] = flag(column == as_column(row))
    for part in range(PARTS):
        span = slice(part * PART, (part + 1) * PART)
        same = column[span] == marks[:, span]
        mask = flag(same & (iota((PART, LANES), 0) >= iota((PART, LANES), 1))).astype(BF16)
        causal_ref[part] = jnp.concatenate([mask] * 2, axis=1)
        last = marks[:, (part + 1) * PART - 1 : (part + 1) * PART]
        chosen_ref[part] = jnp.broadcast_to(flag(marks[:, span] == last), (LANES, PART)).astype(BF16)
    follow_ref[...] = flag(column[PART:] == marks[:, PART - 1 : PART]).astype(BF16)
    enter_ref[...] = flag(column == before[:, tokens - 1 :]).astype(BF16)
    inside = spots_ref[block * lines + PART // LANES - 1, LANES - 1] == end_of(block)
    weights_ref[ROUNDS + 3 * number] = jnp.where(inside, 1.0, 0.0)
    tail.wait()
    for stream in range(3):
        tail_ref[stream] = ends_ref[stream, 16 - (SHORT - 1) :, :]


def start_copies(x_ref, origin, moves, sems):
    copies = []
    for stream, ref in moves:
        rows = ref.shape[0] // COPIES
        for number in range(COPIES):
            span = slice(number * rows, (number + 1) * rows)
            there = pl.ds(pl.multiple_of(origin, ref.shape[1]), ref.shape[1])
            copies.append(
                pltpu.make_async_copy(x_ref.at[stream, span, there], ref.at[span, :], sems.at[len(copies)])
            )
            copies[-1].start()
    return copies


def lag_kernel(*refs, side):
    copies = []
    if side == OWN:
        place_ref, x_ref, pack_ref, taps_ref, fall_ref, keys_ref, values_ref, sems = refs
        copies = start_copies(x_ref, place_ref[OWN], ((1, keys_ref), (2, values_ref)), sems)
    else:
        pack_ref, taps_ref, fall_ref = refs
    left = (PART - 1 - iota((LANES, PART), 1)).astype(F32)

    def tile(number, carried):
        at = lanes_at(number * LANES)
        fall = jnp.exp2(as_column(pack_ref[RATE : RATE + 1, at] * -LOG2E) * left)
        fall_ref[pl.ds(pl.multiple_of(number * LANES, LANES), LANES), :] = fall.astype(BF16)
        terms = (as_column(pack_ref[GAIN : GAIN + 1, at]) * fall).reshape(TILE_GROUPS, MODES, PART)
        groups = pl.ds(pl.multiple_of(number * TILE_GROUPS, TILE_GROUPS), TILE_GROUPS)
        taps_ref[groups, :] = jnp.sum(terms, axis=1)
        return carried

    lax.fori_loop(0, pack_ref.shape[1] // LANES, tile, 0, unroll=4)
    for copy in copies:
        copy.wait()


def state_kernel(
    place_ref, weights_ref, x_ref, keys_ref, values_ref, halo_ref, pack_ref, fall_ref, agree_ref, chosen_ref,
    gated_ref, query_ref, state_ref, middle_ref, rates_ref, *rest, side, passing,
):
    tokens, channels = gated_ref.shape
    copies = start_copies(x_ref, place_ref[side], ((0, query_ref),), rest[-1])
    if side == OWN:
        copies += start_copies(
            x_ref, place_ref[OTHER], ((1, rest[0]), (2, rest[1])), rest[-1].at[pl.ds(COPIES, 2 * COPIES)]
        )
    origin = place_ref[side]
    shape = (MODES, LANES)
    index = iota(shape, 1) // GROUP * GROUP + iota(shape, 0)

    def feature_jobs(start, made):
        at = lanes_at(start)

        def one(row):
            halos = [halo_ref[stream, :, lanes_at(origin + start)].astype(F32) for stream in (1, 2)]
            key = featured(keys_ref, at, pack_ref[SHORT : 2 * SHORT, at], agree_ref, row, halos[0])
            value = featured(values_ref, at, pack_ref[2 * SHORT : 3 * SHORT, at], agree_ref, row, halos[1])
            made[row] = (key * value).astype(BF16)
            gated_ref[row : row + ROWS, at] = made[row]

        return [lambda row=row: one(row) for row in range(0, tokens, ROWS)]

    def state_jobs(start, made):
        at = lanes_at(start)
        held = {}

        def product(part):
            fall = fall_ref[pl.ds(pl.multiple_of(start, LANES), LANES), :]
            right = [made[row] for row in range(part * PART, (part + 1) * PART, ROWS)]
            held[part] = jnp.dot(
                fall * chosen_ref[part], jnp.concatenate(right, axis=0), preferred_element_type=F32
            )

        def finish():
            first, last = diagonal(held[0]), diagonal(held[1])
            row = jnp.broadcast_to(pack_ref[RATE : RATE + 1, at], shape)
            rate = jnp.take_along_axis(row, index, axis=1)
            rates_ref[:, at] = rate
            middle_ref[:, at] = first
            onward = jnp.exp(-rate * PART) * weights_ref[passing] * first
            state_ref[:, at] = (last + onward).astype(BF16)

        return [lambda part=part: product(part) for part in range(PARTS)] + [finish]

    @pl.loop(0, channels // (TILES * LANES))
    def _(step):
        made, jobs = {}, []
        for tile in range(TILES):
            start = step * TILES * LANES + tile * LANES
            made = {}
            ahead = feature_jobs(start, made)
            weave(ahead, jobs)
            jobs = state_jobs(start, made)
        weave(jobs)

    for copy in copies:
        copy.wait()


def lag_jobs(step, first, taps_ref, mats_ref):
    held = {}

    def bases(tile):
        at = pl.multiple_of((first + step * WIDE) // GROUP, 8) + tile * TILE_GROUPS
        taps = taps_ref[pl.ds(pl.multiple_of(at, 8), TILE_GROUPS), :]
        index = (iota((8, LANES), 1) + (LANES - 1) - iota((8, LANES), 0)) & (LANES - 1)
        rows = [jnp.broadcast_to(taps[group : group + 1], (8, LANES)) for group in range(TILE_GROUPS)]
        early = [jnp.take_along_axis(row, index, axis=1) for row in rows]
        late = [pltpu.roll(base, 8, 1) for base in early]
        held[tile] = [jnp.concatenate(both, axis=0).astype(BF16) for both in zip(early, late)]

    def rolls(tile, row):
        for group in range(TILE_GROUPS):
            both = held[tile][group]
            odd = group % 2
            mats_ref[tile * 4 + group // 2, row : row + 16, odd * LANES : (odd + 1) * LANES] = (
                pltpu.roll(both, row, 1) if row else both
            )

    jobs = []
    for tile in range(WIDE // LANES):
        jobs.append(lambda tile=tile: bases(tile))
        jobs += [lambda tile=tile, row=row: rolls(tile, row) for row in range(0, PART, 16)]
    return jobs


def filter_jobs(
    step, first, gated_ref, pack_ref, middle_ref, mats_ref, causal_ref, follow_ref,
    local_ref, onward_ref,
):
    held = {}
    odd = iota((16, LANES), 1) // GROUP % 2
    keep = [jnp.concatenate([flag(odd == i).astype(BF16)] * (PART // 16), axis=0) for i in (0, 1)]
    own = iota((1, LANES), 1) // (2 * GROUP)

    def source(tile):
        return lanes_at(first + step * WIDE + tile * LANES)

    def target(tile):
        return lanes_at(step * WIDE + tile * LANES)

    def span(part):
        return slice(part * PART, (part + 1) * PART)

    def inner(part, tile):
        values = gated_ref[span(part), source(tile)]
        right = jnp.concatenate([values * keep[0], values * keep[1]], axis=0)
        left = jnp.concatenate([mats_ref[tile * 4 + i] * causal_ref[part] for i in range(4)], axis=0)
        held["full", part, tile] = jnp.dot(left, right, preferred_element_type=F32)

    def pick(part, tile):
        full = held["full", part, tile]
        value = full[:PART]
        for i in range(1, 4):
            value = jnp.where(own == i, full[i * PART : (i + 1) * PART], value)
        held[part, tile] = value

    def carry(tile):
        at = source(tile)
        age = (iota((PART, LANES), 0) + 1).astype(F32)
        onward = jnp.exp2(pack_ref[RATE : RATE + 1, at] * -LOG2E * age) * pack_ref[GAIN : GAIN + 1, at]
        onward = onward.astype(BF16)
        onward_ref[:, target(tile)] = onward
        held["carry", tile] = jnp.dot(
            onward * follow_ref[...], spread(middle_ref[:, at]), preferred_element_type=F32
        )

    def finish(part, tile):
        at = source(tile)
        value = held[part, tile] + pack_ref[SKIP : SKIP + 1, at] * gated_ref[span(part), at].astype(F32)
        if part:
            value = value + held["carry", tile]
        local_ref[span(part), target(tile)] = value

    return [
        lambda: carry(0), lambda: inner(0, 0), lambda: carry(1), lambda: inner(1, 0),
        lambda: pick(0, 0), lambda: finish(0, 0), lambda: inner(0, 1), lambda: pick(1, 0),
        lambda: finish(1, 0), lambda: inner(1, 1), lambda: pick(0, 1), lambda: finish(0, 1),
        lambda: pick(1, 1), lambda: finish(1, 1),
    ]


def local_kernel(
    place_ref, query_ref, halo_ref, gated_ref, pack_ref, taps_ref, middle_ref,
    agree_ref, causal_ref, follow_ref, _,
    local_ref, queries_ref, onward_ref, token_ref,
    mats_a, mats_b, *, side, first,
):
    tokens, channels = local_ref.shape
    token_ref[...] = jnp.zeros_like(token_ref)
    origin = place_ref[side] + first

    def query_jobs(step):
        def one(tile, start):
            at = step * WIDE + tile * LANES
            halo = halo_ref[0, :, lanes_at(origin + at)].astype(F32)
            source = lanes_at(first + at)
            summed = featured(query_ref, source, pack_ref[0:SHORT, source], agree_ref, start, halo)
            queries_ref[start : start + ROWS, lanes_at(at)] = summed.astype(BF16)

        return [
            lambda tile=tile, start=start: one(tile, start)
            for tile in range(2) for start in range(0, tokens, ROWS)
        ]

    def work(step, mats_ref):
        return filter_jobs(
            step, first, gated_ref, pack_ref, middle_ref, mats_ref, causal_ref, follow_ref,
            local_ref, onward_ref,
        )

    chunks = channels // WIDE
    weave(lag_jobs(0, first, taps_ref, mats_a))

    @pl.loop(0, chunks // 2)
    def _(pair):
        step = pair * 2
        weave(work(step, mats_a), lag_jobs(step + 1, first, taps_ref, mats_b), query_jobs(step))
        after = jnp.minimum(step + 2, chunks - 1)
        weave(work(step + 1, mats_b), lag_jobs(after, first, taps_ref, mats_a), query_jobs(step + 1))


def output_kernel(place_ref, enter_ref, *refs, pieces, chunk):
    inputs, (out_ref, held_ref, sems) = refs[:-3], refs[-3:]
    pending = []
    done = 0
    for index, (side, first, count) in enumerate(pieces):
        local_ref, queries_ref, onward_ref = inputs[3 * index : 3 * index + 3]
        carry_ref, rates_ref = inputs[3 * len(pieces) + 2 * side : 3 * len(pieces) + 2 * side + 2]

        def tile(start):
            at, source = lanes_at(start), lanes_at(first + start)
            carry = carry_ref[:, source].astype(F32)
            for part in range(PARTS):
                span = slice(part * PART, (part + 1) * PART)
                if part:
                    carry = carry * jnp.exp(-rates_ref[:, source] * PART)
                carried = jnp.dot(
                    onward_ref[:, at] * enter_ref[span, :], spread(carry), preferred_element_type=F32
                )
                mixed = (local_ref[span, at] + carried).astype(BF16).astype(F32)
                held_ref[span, lanes_at(done + start)] = (
                    queries_ref[span, at].astype(F32) * mixed
                ).astype(BF16)

        for begin in range(0, count, chunk):

            def step(number, carried):
                tile(begin + number * LANES)
                return carried

            lax.fori_loop(0, chunk // LANES, step, 0, unroll=4)
            where = pl.multiple_of(place_ref[side] + (first + begin), chunk)
            copy = pltpu.make_async_copy(
                held_ref.at[:, done + begin : done + begin + chunk],
                out_ref.at[:, pl.ds(where, chunk)],
                sems.at[len(pending)],
            )
            copy.start()
            pending.append(copy)
        done += count
    for copy in pending:
        copy.wait()


def ordered(upper, mine, other):
    mine, other = mine.astype(F32), other.astype(F32)
    return jnp.where(upper, other, mine), jnp.where(upper, mine, other)


def decay(rate, span):
    return jnp.exp(-rate * span)


def pair_kernel(place_ref, weights_ref, kept_ref, got_ref, rate_ref, first_ref, mine_ref, send_ref, *, tokens):
    first, second = ordered(place_ref[LOW] == 1, kept_ref[...], got_ref[...])
    first_ref[...] = first
    ends = second + weights_ref[PAIR_PASS] * decay(rate_ref[...], tokens) * first
    half = ends.shape[1] // 2
    mine, send = ordered(place_ref[HIGH] == 1, ends[:, :half], ends[:, half:])
    mine_ref[...] = mine
    send_ref[...] = send.astype(BF16)


def narrowed(place_ref, rate_ref):
    half = rate_ref.shape[1] // 2
    return jnp.where(place_ref[HIGH] == 1, rate_ref[:, half:], rate_ref[:, :half])


def quad_kernel(place_ref, weights_ref, mine_ref, got_ref, rate_ref, lower_ref, total_ref, send_ref, *, tokens):
    lower, upper = ordered(place_ref[HIGH] == 1, mine_ref[...], got_ref[...])
    rate = narrowed(place_ref, rate_ref)
    lower_ref[...] = lower
    total = upper + weights_ref[QUAD_PASS] * decay(rate, 2 * tokens) * lower
    total_ref[...] = total
    send_ref[...] = total.astype(BF16)


def round_kernel(place_ref, weights_ref, total_ref, got_ref, rate_ref, *refs, tokens, number, last):
    rate = narrowed(place_ref, rate_ref)
    got = got_ref[...].astype(F32)
    at = ROUNDS + 3 * number
    carry = weights_ref[at] * decay(rate, weights_ref[at + 1]) * got
    if number:
        carry, refs = refs[0][...] + carry, refs[1:]
    if not last:
        carry_ref, sum_ref, send_ref = refs
        carry_ref[...] = carry
        before, after = ordered(place_ref[UPSIDES + number] == 1, total_ref[...], got)
        total = after + weights_ref[at + 2] * decay(rate, (4 << number) * tokens) * before
        sum_ref[...] = total
        send_ref[...] = total.astype(BF16)
        return
    lower_ref, keep_ref, send_ref = refs
    ahead = lower_ref[...] + weights_ref[QUAD_FROM] * decay(rate, 2 * tokens) * carry
    keep, send = ordered(place_ref[HIGH] == 1, carry, ahead)
    keep_ref[...] = keep
    send_ref[...] = send.astype(BF16)


def back_kernel(place_ref, weights_ref, mine_ref, got_ref, rate_ref, first_ref, keep_ref, send_ref, *, tokens):
    carry = jnp.concatenate(ordered(place_ref[HIGH] == 1, mine_ref[...], got_ref[...]), axis=1)
    ahead = first_ref[...] + weights_ref[PAIR_FROM] * decay(rate_ref[...], tokens) * carry
    keep, send = ordered(place_ref[LOW] == 1, carry, ahead)
    keep_ref[...] = keep.astype(BF16)
    send_ref[...] = send.astype(BF16)


def params(mebibytes=20):
    return pltpu.CompilerParams(vmem_limit_bytes=mebibytes * 1024 * 1024)


def cost(flops, size):
    return pl.CostEstimate(flops=flops, bytes_accessed=size, transcendentals=0)


def shaped(shape, dtype):
    return jax.ShapeDtypeStruct(shape, dtype)


def small_call(kernel, name, place, weights, *operands, outs, tokens_before=(), **static):
    waits = len(tokens_before)
    return pl.pallas_call(
        lambda *refs: kernel(*refs[waits:], **static),
        in_specs=[ANY] * waits + [SMEM, SMEM] + [VMEM] * len(operands),
        out_specs=[VMEM] * len(outs),
        out_shape=outs,
        compiler_params=params(),
        cost_estimate=cost(1 << 18, 1 << 18),
        name=name,
    )(*tokens_before, place, weights, *operands)


def placing(segments, weights, streams, devices, fsdp_count):
    _, tokens, channels = streams.shape
    marks = segments.reshape(-1, LANES)
    short, skip, rates, residues = weights
    owned = short.shape[2]
    arrays = (marks, short, skip.reshape(1, owned), rates.T, residues.T)

    def whole(array):
        return pl.BlockSpec(array.shape, lambda i: (0,) * len(array.shape))

    outs = [
        shaped((16,), jnp.int32),
        shaped((32,), F32),
        shaped((SHORT - 1, tokens, LANES), F32),
        shaped((PARTS, PART, WIDE), BF16),
        shaped((PART, LANES), BF16),
        shaped((tokens, LANES), BF16),
        shaped((PARTS, LANES, PART), BF16),
        shaped((PACKED, owned), F32),
        shaped((3, SHORT - 1, channels), BF16),
    ]
    return pl.pallas_call(
        lambda *refs: place_kernel(*refs, devices=devices, tokens=tokens, fsdp_count=fsdp_count),
        grid=(1,),
        in_specs=[SMEM] + [whole(array) for array in arrays] + [HBM],
        out_specs=[SMEM, SMEM] + [whole(out) for out in outs[2:]],
        out_shape=outs,
        scratch_shapes=[pltpu.VMEM((3, 16, channels), BF16), pltpu.SemaphoreType.DMA],
        compiler_params=params(54),
        cost_estimate=cost(1 << 20, 1 << 20),
        name="placing",
    )(marks, *arrays, streams)


def lags(place, streams, pack, side, name):
    _, tokens, _ = streams.shape
    channels = pack.shape[1]
    outs = [shaped((channels // GROUP, PART), F32), shaped((channels, PART), BF16)]
    operands, specs, scratch = [pack], [VMEM], []
    if side == OWN:
        outs += [shaped((tokens, channels), BF16)] * 2
        operands, specs = [place, streams, pack], [SMEM, HBM, VMEM]
        scratch = [pltpu.SemaphoreType.DMA((2 * COPIES,))]
    return pl.pallas_call(
        lambda *refs: lag_kernel(*refs, side=side),
        in_specs=specs,
        out_specs=[VMEM] * len(outs),
        out_shape=outs,
        scratch_shapes=scratch,
        compiler_params=params(46 if side == OWN else 20),
        cost_estimate=cost(10 * channels * PART, 16 * channels * PART),
        name="lags_" + name,
    )(*operands)


def block_states(place, weights, streams, operands, side, passing, name):
    _, tokens, _ = streams.shape
    channels = operands[0].shape[1]
    outs = [
        shaped((tokens, channels), BF16),
        shaped((tokens, channels), BF16),
        shaped((MODES, channels), BF16),
        shaped((MODES, channels), F32),
        shaped((MODES, channels), F32),
    ]
    if side == OWN:
        outs += [shaped((tokens, channels), BF16)] * 2
    return pl.pallas_call(
        lambda *refs: state_kernel(*refs, side=side, passing=passing),
        in_specs=[SMEM, SMEM, HBM] + [VMEM] * len(operands),
        out_specs=[VMEM] * len(outs),
        out_shape=outs,
        scratch_shapes=[pltpu.SemaphoreType.DMA((3 * COPIES,))],
        compiler_params=params(40),
        cost_estimate=cost(20 * tokens * channels, 16 * tokens * channels),
        name="block_states_" + name,
    )(place, weights, streams, *operands)


def block_local(place, operands, after, side, first, count, name):
    tokens = operands[0].shape[0]
    return pl.pallas_call(
        lambda *refs: local_kernel(*refs, side=side, first=first),
        in_specs=[SMEM] + [VMEM] * len(operands) + [ANY],
        out_specs=[VMEM] * 4,
        out_shape=[
            shaped((tokens, count), F32),
            shaped((tokens, count), BF16),
            shaped((PART, count), BF16),
            shaped((8, LANES), F32),
        ],
        scratch_shapes=[
            pltpu.VMEM((WIDE // GROUP // 2, PART, WIDE), BF16),
            pltpu.VMEM((WIDE // GROUP // 2, PART, WIDE), BF16),
        ],
        compiler_params=params(),
        cost_estimate=cost(2 * PART * PART * 2 * count * TILE_GROUPS, 40 * tokens * count),
        name="block_local_" + name,
    )(place, *operands, after)


def block_output(place, enter, pieces, locals_, carries, tokens, channels):
    chunk = 1024
    return pl.pallas_call(
        lambda *refs: output_kernel(*refs, pieces=pieces, chunk=chunk),
        in_specs=[SMEM] + [VMEM] * (1 + len(locals_) + len(carries)),
        out_specs=HBM,
        out_shape=shaped((tokens, channels), BF16),
        scratch_shapes=[
            pltpu.VMEM((tokens, channels), BF16),
            pltpu.SemaphoreType.DMA((channels // chunk,)),
        ],
        compiler_params=params(),
        cost_estimate=cost(20 * tokens * channels, 8 * tokens * channels),
        name="block_output",
    )(place, enter, *locals_, *carries)


SPAN = 8


def shifted_2(block, axis, distance):
    devices = range(lax.axis_size(axis))
    route = [(i - distance, i) for i in devices if i - distance in devices]
    return lax.ppermute(block, axis, route)


def contract(pattern, left_side, right_side):
    return jnp.einsum(pattern, left_side, right_side, precision=lax.Precision.HIGHEST)


def featurize(block_rows, before_rows, tap_rows, row_marks, before_marks):
    margin = before_rows.shape[1]
    row_count = block_rows.shape[1]
    joined = jnp.concatenate([before_rows, block_rows], axis=1)
    all_marks = jnp.concatenate([before_marks, row_marks])
    summed = block_rows.astype(jnp.float32) * tap_rows[:, 0][:, None, :]
    for offset in range(1, margin + 1):
        shifted = joined[:, margin - offset : margin - offset + row_count].astype(jnp.float32)
        agreeing = all_marks[margin - offset : margin - offset + row_count] == row_marks
        summed = (
            summed
            + jnp.where(agreeing[None, :, None], shifted, 0.0) * tap_rows[:, offset][:, None, :]
        )
    queries = summed[0].astype(jnp.bfloat16)
    gated_prod = (summed[1] * summed[2]).astype(jnp.bfloat16)
    return lax.optimization_barrier((queries, gated_prod))


def tile_filter(gated_prod, tile_marks, decay_rates, mode_gain, rising):
    tile_rows, channels = gated_prod.shape
    groups = channels // GROUP
    block_len = min(128, tile_rows)
    offsets = jnp.arange(block_len, dtype=jnp.float32)
    forward = mode_gain[:, :, None] * jnp.exp(-decay_rates[:, :, None] * offsets)
    backward = jnp.exp(decay_rates[:, :, None] * offsets)
    causal = (offsets[:, None] >= offsets[None, :]).astype(jnp.float32)
    kernel = contract("gmt,gms->gts", forward, backward) * causal
    mode_rates = decay_rates.T[:, :, None]
    closing = jnp.exp(-mode_rates * (block_len - 1.0 - offsets))
    through = jnp.exp(-mode_rates * block_len)
    head_rising = rising[:, :, :block_len]
    values = gated_prod.astype(jnp.float32).reshape(tile_rows, groups, GROUP)
    carried = jnp.zeros((MODES, groups, GROUP), jnp.float32)
    last_seen = jnp.int32(-1)
    pieces = []
    for number in range(tile_rows // block_len):
        block_vals = values[number * block_len : (number + 1) * block_len]
        block_marks = tile_marks[number * block_len : (number + 1) * block_len]
        agreeing = (block_marks[:, None] == block_marks[None, :]).astype(jnp.float32)
        inside = contract("gts,sgc->tgc", kernel * agreeing, block_vals)
        follow = (block_marks == last_seen).astype(jnp.float32)
        inside = inside + follow[:, None, None] * contract("mgt,mgc->tgc", head_rising, carried)
        ending = (block_marks == block_marks[block_len - 1]).astype(jnp.float32)
        fresh_state = contract("mgs,sgc->mgc", closing * ending, block_vals)
        passing = (block_marks[block_len - 1] == last_seen).astype(jnp.float32)
        carried = fresh_state + passing * through * carried
        last_seen = block_marks[block_len - 1]
        pieces.append(inside)
    return (jnp.concatenate(pieces, axis=0), carried)


def narrow_local(streams, segments, short_taps, decay_rates, residues, skip_gain):
    fsdp_count = lax.axis_size("fsdp")
    ctx_count = lax.axis_size("ctx")
    tile_index = lax.axis_index("ctx")
    own_rows = streams.shape[1]
    tile_rows = own_rows * fsdp_count
    margin = SHORT - 1
    padded_marks = jnp.concatenate([jnp.full((margin,), -1, jnp.int32), segments])
    tile_start = tile_index * tile_rows
    tile_marks = lax.dynamic_slice_in_dim(segments, tile_start, tile_rows)
    local_streams = lax.all_to_all(streams, "fsdp", split_axis=2, concat_axis=1, tiled=True)
    before_rows = shifted_2(local_streams[:, tile_rows - margin :, :], "ctx", 1)
    before_marks = lax.dynamic_slice_in_dim(padded_marks, tile_start, margin)
    queries, gated_prod = featurize(
        local_streams, before_rows, short_taps, tile_marks, before_marks
    )
    channels = gated_prod.shape[1]
    groups = channels // GROUP
    mode_gain = residues * jnp.sqrt(-jnp.expm1(-2.0 * decay_rates))
    positions = jnp.arange(tile_rows, dtype=jnp.float32)
    mode_rates = decay_rates.T[:, :, None]
    rising = mode_gain.T[:, :, None] * jnp.exp(-mode_rates * (positions + 1.0))
    local_part, end_state = tile_filter(gated_prod, tile_marks, decay_rates, mode_gain, rising)
    first_mark = tile_marks[0]
    falling = jnp.exp(-mode_rates * (tile_rows - 1.0 - positions))

    def source_state(operand):
        source_vals, source_marks = operand
        chosen = (source_marks == first_mark).astype(jnp.float32)
        return contract(
            "mgs,sgc->mgc",
            falling * chosen,
            source_vals.astype(jnp.float32).reshape(tile_rows, groups, GROUP),
        )

    def empty_state(operand):
        return jnp.zeros((MODES, groups, GROUP), jnp.float32)

    prior_state = jnp.zeros((MODES, groups, GROUP), jnp.float32)
    for distance in range(1, min(SPAN, ctx_count - 1) + 1):
        source_tile = shifted_2(gated_prod, "ctx", distance)
        source_index = tile_index - distance
        source_marks = lax.dynamic_slice_in_dim(
            segments, jnp.maximum(source_index, 0) * tile_rows, tile_rows
        )
        paired = (source_index >= 0) & (source_marks[tile_rows - 1] == first_mark)
        received = lax.cond(paired, source_state, empty_state, (source_tile, source_marks))
        prior_state = prior_state + jnp.exp(-mode_rates * ((distance - 1) * tile_rows)) * received
    prior_mark = first_mark.astype(jnp.float32)
    follow_tile = (tile_marks.astype(jnp.float32) == prior_mark).astype(jnp.float32)
    filtered = local_part + follow_tile[:, None, None] * contract(
        "mgt,mgc->tgc", rising, prior_state
    )
    mixed_out = (
        filtered.reshape(tile_rows, channels) + skip_gain * gated_prod.astype(jnp.float32)
    ).astype(jnp.bfloat16)
    mixed_out = lax.optimization_barrier(mixed_out)
    payload = (queries.astype(jnp.float32) * mixed_out.astype(jnp.float32)).astype(jnp.bfloat16)
    returned = lax.all_to_all(payload, "fsdp", split_axis=0, concat_axis=1, tiled=True)
    return returned


def swap(array, distance, devices):
    route = [(i, i ^ distance) for i in range(devices)]
    return lax.ppermute(array, ("ctx", "fsdp"), route)


def carry_in(place, weights, sent, kept, rate, devices, tokens, beside):
    full, half = kept.shape, (kept.shape[0], kept.shape[1] // 2)
    wide, narrow, lean = shaped(full, F32), shaped(half, F32), shaped(half, BF16)

    def call(kernel, name, send, distance, *operands, outs, **static):
        got = swap(send, distance, devices)
        return small_call(
            kernel, name, place, weights, operands[0], got, rate, *operands[1:], outs=outs, tokens=tokens,
            tokens_before=beside(name, send), **static,
        )

    first, mine, send = call(pair_kernel, "pairs", sent, 1, kept, outs=[wide, narrow, lean])
    lower, total, send = call(quad_kernel, "quads", send, 2, mine, outs=[narrow, narrow, lean])
    carry, number, size = [], 0, 4
    while size < devices:
        name = "round" + str(number)
        if 2 * size < devices:
            held, total, send = call(
                round_kernel, name, send, size, total, *carry, outs=[narrow, narrow, lean],
                number=number, last=False,
            )
            carry = [held]
        else:
            keep, send = call(
                round_kernel, name, send, size, total, *carry, lower, outs=[narrow, lean],
                number=number, last=True,
            )
        size, number = 2 * size, number + 1
    full_lean = shaped(full, BF16)
    keep, send = call(back_kernel, "back", send, 2, keep, first, outs=[full_lean, full_lean])
    beside("end", send)
    return swap(send, 1, devices), keep


def local(streams, segments, short_taps, decay_rates, residues, skip_gain):
    fsdp_count, ctx_count = lax.axis_size("fsdp"), lax.axis_size("ctx")
    devices = fsdp_count * ctx_count
    _, tokens, channels = streams.shape
    if tokens != PARTS * PART or fsdp_count != 2 or devices < 8:
        return narrow_local(streams, segments, short_taps, decay_rates, residues, skip_gain)
    owned = short_taps.shape[2]
    place, weights, agree, causal, follow, enter, chosen, own_pack, tail = placing(
        segments, (short_taps, skip_gain, decay_rates, residues), streams, devices, fsdp_count
    )
    halo = lax.ppermute(tail, ("ctx", "fsdp"), [(i, i + 1) for i in range(devices - 1)])
    other_pack = lax.ppermute(own_pack, "fsdp", [(0, 1), (1, 0)])
    passing = ROUNDS + 3 * ((devices // 4).bit_length() - 1)
    found, brought = [], ()
    for side, (name, pack) in enumerate((("own", own_pack), ("other", other_pack))):
        taps, fall, *loaded = lags(place, streams, pack, side, name)
        brought = loaded or brought
        gated, query, state, middle, spread_rates, *brought = block_states(
            place, weights, streams, (*brought, halo, pack, fall, agree, chosen), side, passing, name
        )
        operands = (query, halo, gated, pack, taps, middle, agree, causal, follow)
        found.append((operands, state, spread_rates))
    span = owned // 2
    pieces = [(side, first, span) for side in (OWN, OTHER) for first in range(0, owned, span)]
    beside_rounds = {"round0": 1, "round1": 1, "round2": 1}
    waiting, locals_ = list(pieces), []

    def beside(name, array):
        count = len(waiting) if name == "end" else beside_rounds.get(name, 0)
        given = []
        for _ in range(min(count, len(waiting))):
            side, first, size = waiting.pop(0)
            label = "own" if side == OWN else "other"
            *made, token = block_local(
                place, found[side][0], array, side, first, size, label + str(first // size)
            )
            locals_.extend(made)
            given.append(token)
        return given

    carries = carry_in(
        place, weights, found[0][1], found[1][1], found[1][2], devices, tokens, beside
    )
    sides = [carries[0], found[0][2], carries[1], found[1][2]]
    return block_output(place, enter, pieces, locals_, sides, tokens, channels)


def solution(mesh):
    placed = (
        P(None, ("ctx", "fsdp"), None),
        P(),
        P(None, None, "fsdp"),
        P("fsdp", None),
        P("fsdp", None),
        P("fsdp"),
    )
    return jax.shard_map(
        local, mesh=mesh, in_specs=placed, out_specs=P(("ctx", "fsdp"), None), check_vma=False
    )
```

```python
import jax
import jax.numpy as jnp
from jax import lax
from jax.experimental import pallas as pl
from jax.experimental.pallas import tpu as pltpu
from jax.sharding import PartitionSpec as P

GROUP = 16
MODES = 16
SHORT = 3
LANES = 128
PART = 128
PARTS = 2
WIDE = 256
COPIES = 4
TILES = 8
TILE_GROUPS = LANES // GROUP
ROWS = 64
LOG2E = 1.4426950408889634
F32 = jnp.float32
BF16 = jnp.bfloat16
VMEM = pl.BlockSpec(memory_space=pltpu.VMEM)
SMEM = pl.BlockSpec(memory_space=pltpu.SMEM)
HBM = pl.BlockSpec(memory_space=pltpu.HBM)
ANY = pl.BlockSpec(memory_space=pl.ANY)
SKIP, RATE, GAIN, PACKED = 9, 10, 11, 16
OWN, OTHER, LOW, HIGH, UPSIDES = 0, 1, 2, 3, 4
PAIR_PASS, QUAD_PASS, QUAD_FROM, PAIR_FROM, ROUNDS = 0, 1, 2, 3, 4
ROWS_OF_PLACE, PLACES = 32, 16


def iota(shape, axis):
    return lax.broadcasted_iota(jnp.int32, shape, axis)


def flag(condition):
    return jnp.where(condition, 1.0, 0.0)


def as_column(row):
    return jnp.transpose(jnp.broadcast_to(row, (LANES, row.shape[1])))


def lanes_at(start, size=LANES):
    return pl.ds(pl.multiple_of(start, LANES), size)


def weave(*lists):
    order = sorted(
        ((i + 0.5) / len(jobs), n, i) for n, jobs in enumerate(lists) for i in range(len(jobs))
    )
    for _, n, i in order:
        lists[n][i]()


def featured(x_ref, lanes, taps, agree_ref, start, halo):
    if start == 0:
        here = x_ref[0:ROWS, lanes].astype(F32)
        sub = iota((8, LANES), 0)
        ahead = jnp.where(sub == 6, halo[0:1], jnp.where(sub == 7, halo[1:2], 0.0))
    else:
        both = x_ref[start - 16 : start + ROWS, lanes].astype(F32)
        here, ahead = both[16:], both[8:16]
    joined = jnp.concatenate([ahead, here], axis=0)
    summed = here * taps[0:1]
    for offset in range(1, SHORT):
        shifted = pltpu.roll(joined, offset, 0)[8:]
        agree = agree_ref[offset - 1, start : start + ROWS, :]
        summed = summed + shifted * agree * taps[offset : offset + 1]
    return summed


def spread(state):
    own = iota(state.shape, 1) // GROUP
    return jnp.concatenate(
        [jnp.where(own == group, state, 0.0) for group in range(TILE_GROUPS)], axis=0
    ).astype(BF16)


def diagonal(full):
    own = iota((MODES, LANES), 1) // GROUP
    state = full[:MODES]
    for group in range(1, TILE_GROUPS):
        state = jnp.where(own == group, full[group * MODES : (group + 1) * MODES], state)
    return state


def packing_kernel(*refs):
    sources, pack_ref, held, sems = refs[1:5], refs[5], refs[6:10], refs[10]
    short_ref, skip_ref, rates_ref, residues_ref = held
    copies = [
        pltpu.make_async_copy(source, target, sems.at[number])
        for number, (source, target) in enumerate(zip(sources, held))
    ]
    for copy in copies:
        copy.start()
    for copy in copies:
        copy.wait()
    for stream in range(3):
        pack_ref[stream * SHORT : (stream + 1) * SHORT, :] = short_ref[stream]
    pack_ref[SKIP : SKIP + 1, :] = skip_ref[...]
    pack_ref[GAIN + 1 :, :] = jnp.zeros((PACKED - GAIN - 1, pack_ref.shape[1]), F32)
    shape = (MODES, LANES)
    own = iota(shape, 1) % MODES == iota(shape, 0)

    def tile(number, carried):
        at = lanes_at(number * LANES)
        first = number * TILE_GROUPS
        source = lanes_at(first // LANES * LANES)
        index = first % LANES + iota(shape, 1) // MODES
        rate = jnp.take_along_axis(rates_ref[:, source], index, axis=1)
        factor = jnp.take_along_axis(residues_ref[:, source], index, axis=1)
        rate = jnp.sum(jnp.where(own, rate, 0.0), axis=0, keepdims=True)
        factor = jnp.sum(jnp.where(own, factor, 0.0), axis=0, keepdims=True)
        half = jnp.tanh(rate)
        pack_ref[RATE : RATE + 1, at] = rate
        pack_ref[GAIN : GAIN + 1, at] = factor * jnp.sqrt(2.0 * half / (1.0 + half))
        return carried

    lax.fori_loop(0, pack_ref.shape[1] // LANES, tile, 0, unroll=4)


def place_kernel(
    x_ref, spots_ref, marks_ref,
    place_ref, weights_ref, rows_ref, agree_ref, causal_ref, follow_ref, enter_ref, chosen_ref, keys_ref,
    held_ref, sem, moves, *, devices, tokens, fsdp_count,
):
    copy = pltpu.make_async_copy(marks_ref, held_ref, sem)
    copy.start()
    owned = keys_ref.shape[1]
    lines = tokens // LANES
    fsdp_index = lax.axis_index("fsdp")
    block = lax.axis_index("ctx") * fsdp_count + fsdp_index
    brought = start_copies(x_ref, fsdp_index * owned, ((1, keys_ref),), moves)
    place_ref[OWN] = fsdp_index * owned
    place_ref[OTHER] = (1 - fsdp_index) * owned
    place_ref[LOW] = lax.rem(block, 2)
    place_ref[HIGH] = lax.rem(lax.div(block, 2), 2)
    pair = block - lax.rem(block, 2)
    quad = block - lax.rem(block, 4)

    def end_of(index):
        return spots_ref[jnp.maximum(index, 0) * lines + lines - 1, LANES - 1]

    def passes(earlier, later):
        return jnp.where(end_of(earlier) == end_of(later), 1.0, 0.0)

    weights_ref[PAIR_PASS] = passes(pair, pair + 1)
    weights_ref[QUAD_PASS] = passes(quad + 1, quad + 3)
    weights_ref[QUAD_FROM] = passes(quad - 1, quad + 1)
    weights_ref[PAIR_FROM] = passes(pair - 1, pair)
    size, number = 4, 0
    while size < devices:
        start = block - lax.rem(block, 2 * size)
        upside = lax.rem(lax.div(block, size), 2)
        middle = start + size - 1
        place_ref[UPSIDES + number] = upside
        at = ROUNDS + 3 * number
        weights_ref[at] = jnp.where(upside == 1, passes(middle, quad - 1), 0.0)
        weights_ref[at + 1] = (jnp.maximum(quad - 1 - middle, 0) * tokens).astype(F32)
        weights_ref[at + 2] = passes(middle, middle + size)
        size, number = 2 * size, number + 1

    copy.wait()

    def marks_of(index):
        return jnp.concatenate(
            [held_ref[pl.ds(index * lines + line, 1), :] for line in range(lines)], axis=1
        ).astype(F32)

    marks = marks_of(block)
    before = jnp.where(block > 0, marks_of(jnp.maximum(block - 1, 0)), -1.0)
    column = as_column(marks)
    lane = iota(marks.shape, 1)
    for offset in range(1, SHORT):
        row = jnp.where(lane < offset, pltpu.roll(before, offset, 1), pltpu.roll(marks, offset, 1))
        agree_ref[offset - 1] = flag(column == as_column(row))
    for part in range(PARTS):
        span = slice(part * PART, (part + 1) * PART)
        same = column[span] == marks[:, span]
        mask = flag(same & (iota((PART, LANES), 0) >= iota((PART, LANES), 1))).astype(BF16)
        causal_ref[part] = jnp.concatenate([mask] * 2, axis=1)
        last = marks[:, (part + 1) * PART - 1 : (part + 1) * PART]
        chosen_ref[part] = jnp.broadcast_to(flag(marks[:, span] == last), (LANES, PART)).astype(BF16)
    follow_ref[...] = flag(column[PART:] == marks[:, PART - 1 : PART]).astype(BF16)
    enter_ref[...] = flag(column == before[:, tokens - 1 :]).astype(BF16)
    inside = spots_ref[block * lines + PART // LANES - 1, LANES - 1] == end_of(block)
    weights_ref[ROUNDS + 3 * number] = jnp.where(inside, 1.0, 0.0)
    for spare in range(ROUNDS + 3 * number + 1, ROWS_OF_PLACE):
        weights_ref[spare] = 0.0
    for spare in range(UPSIDES + number, PLACES):
        place_ref[spare] = 0
    for number in range(rows_ref.shape[0]):
        value = weights_ref[number] if number < ROWS_OF_PLACE else place_ref[number - ROWS_OF_PLACE].astype(F32)
        rows_ref[number : number + 1, :] = jnp.full((1, LANES), value, F32)
    for copy in brought:
        copy.wait()


def start_copies(x_ref, origin, moves, sems):
    copies = []
    for stream, ref in moves:
        rows = ref.shape[0] // COPIES
        for number in range(COPIES):
            span = slice(number * rows, (number + 1) * rows)
            there = pl.ds(pl.multiple_of(origin, ref.shape[1]), ref.shape[1])
            copies.append(
                pltpu.make_async_copy(x_ref.at[stream, span, there], ref.at[span, :], sems.at[len(copies)])
            )
            copies[-1].start()
    return copies


def lag_kernel(*refs, side):
    copies = []
    if side == OWN:
        place_ref, x_ref, pack_ref, taps_ref, fall_ref, values_ref, sems = refs
        copies = start_copies(x_ref, place_ref[OWN], ((2, values_ref),), sems)
    else:
        pack_ref, taps_ref, fall_ref = refs
    left = (PART - 1 - iota((LANES, PART), 1)).astype(F32)

    def tile(number, carried):
        at = lanes_at(number * LANES)
        fall = jnp.exp2(as_column(pack_ref[RATE : RATE + 1, at] * -LOG2E) * left)
        fall_ref[pl.ds(pl.multiple_of(number * LANES, LANES), LANES), :] = fall.astype(BF16)
        terms = (as_column(pack_ref[GAIN : GAIN + 1, at]) * fall).reshape(TILE_GROUPS, MODES, PART)
        groups = pl.ds(pl.multiple_of(number * TILE_GROUPS, TILE_GROUPS), TILE_GROUPS)
        taps_ref[groups, :] = jnp.sum(terms, axis=1)
        return carried

    lax.fori_loop(0, pack_ref.shape[1] // LANES, tile, 0, unroll=4)
    for copy in copies:
        copy.wait()


def state_kernel(
    place_ref, weights_ref, x_ref, keys_ref, values_ref, halo_ref, pack_ref, fall_ref, agree_ref, chosen_ref,
    gated_ref, query_ref, state_ref, middle_ref, rates_ref, *rest, side, passing,
):
    tokens, channels = gated_ref.shape
    copies = start_copies(x_ref, place_ref[side], ((0, query_ref),), rest[-1])
    if side == OWN:
        copies += start_copies(x_ref, place_ref[OTHER], ((1, rest[0]), (2, rest[1])), rest[2])
    origin = place_ref[side]
    shape = (MODES, LANES)
    index = iota(shape, 1) // GROUP * GROUP + iota(shape, 0)

    def feature_jobs(start, made):
        at = lanes_at(start)

        def one(row):
            halos = [halo_ref[stream, :, lanes_at(origin + start)].astype(F32) for stream in (1, 2)]
            key = featured(keys_ref, at, pack_ref[SHORT : 2 * SHORT, at], agree_ref, row, halos[0])
            value = featured(values_ref, at, pack_ref[2 * SHORT : 3 * SHORT, at], agree_ref, row, halos[1])
            made[row] = (key * value).astype(BF16)
            gated_ref[row : row + ROWS, at] = made[row]

        return [lambda row=row: one(row) for row in range(0, tokens, ROWS)]

    def state_jobs(start, made):
        at = lanes_at(start)
        held = {}

        def product(part):
            fall = fall_ref[pl.ds(pl.multiple_of(start, LANES), LANES), :]
            right = [made[row] for row in range(part * PART, (part + 1) * PART, ROWS)]
            held[part] = jnp.dot(
                fall * chosen_ref[part], jnp.concatenate(right, axis=0), preferred_element_type=F32
            )

        def finish():
            first, last = diagonal(held[0]), diagonal(held[1])
            row = jnp.broadcast_to(pack_ref[RATE : RATE + 1, at], shape)
            rate = jnp.take_along_axis(row, index, axis=1)
            rates_ref[:, at] = rate
            middle_ref[:, at] = first
            onward = jnp.exp(-rate * PART) * weights_ref[passing] * first
            state_ref[:, at] = (last + onward).astype(BF16)

        return [lambda part=part: product(part) for part in range(PARTS)] + [finish]

    @pl.loop(0, channels // (TILES * LANES))
    def _(step):
        made, jobs = {}, []
        for tile in range(TILES):
            start = step * TILES * LANES + tile * LANES
            made = {}
            ahead = feature_jobs(start, made)
            weave(ahead, jobs)
            jobs = state_jobs(start, made)
        weave(jobs)

    for copy in copies:
        copy.wait()


def lag_jobs(step, first, taps_ref, mats_ref):
    held = {}

    def bases(tile):
        at = pl.multiple_of((first + step * WIDE) // GROUP, 8) + tile * TILE_GROUPS
        taps = taps_ref[pl.ds(pl.multiple_of(at, 8), TILE_GROUPS), :]
        index = (iota((8, LANES), 1) + (LANES - 1) - iota((8, LANES), 0)) & (LANES - 1)
        rows = [jnp.broadcast_to(taps[group : group + 1], (8, LANES)) for group in range(TILE_GROUPS)]
        early = [jnp.take_along_axis(row, index, axis=1) for row in rows]
        late = [pltpu.roll(base, 8, 1) for base in early]
        held[tile] = [jnp.concatenate(both, axis=0).astype(BF16) for both in zip(early, late)]

    def rolls(tile, row):
        for group in range(TILE_GROUPS):
            both = held[tile][group]
            odd = group % 2
            mats_ref[tile * 4 + group // 2, row : row + 16, odd * LANES : (odd + 1) * LANES] = (
                pltpu.roll(both, row, 1) if row else both
            )

    jobs = []
    for tile in range(WIDE // LANES):
        jobs.append(lambda tile=tile: bases(tile))
        jobs += [lambda tile=tile, row=row: rolls(tile, row) for row in range(0, PART, 16)]
    return jobs


def filter_jobs(
    step, first, gated_ref, pack_ref, middle_ref, mats_ref, causal_ref, follow_ref,
    local_ref, onward_ref,
):
    held = {}
    odd = iota((16, WIDE), 1) // GROUP % 2
    keep = [jnp.concatenate([flag(odd == i).astype(BF16)] * (PART // 16), axis=0) for i in (0, 1)]
    own = iota((1, LANES), 1) // (2 * GROUP)

    def source(tile):
        return lanes_at(first + step * WIDE + tile * LANES)

    def target(tile):
        return lanes_at(step * WIDE + tile * LANES)

    def span(part):
        return slice(part * PART, (part + 1) * PART)

    def inner(part):
        values = gated_ref[span(part), lanes_at(first + step * WIDE, WIDE)]
        right = jnp.concatenate([values * keep[0], values * keep[1]], axis=0)
        for pair in range(WIDE // GROUP // 2):
            held["full", part, pair] = jnp.dot(
                mats_ref[pair] * causal_ref[part], right, preferred_element_type=F32
            )

    def pick(part, tile):
        value = None
        for i in range(4):
            piece = held["full", part, tile * 4 + i][:, tile * LANES : (tile + 1) * LANES]
            value = piece if value is None else jnp.where(own == i, piece, value)
        held[part, tile] = value

    def carry(tile):
        at = source(tile)
        age = (iota((PART, LANES), 0) + 1).astype(F32)
        onward = jnp.exp2(pack_ref[RATE : RATE + 1, at] * -LOG2E * age) * pack_ref[GAIN : GAIN + 1, at]
        onward = onward.astype(BF16)
        onward_ref[:, target(tile)] = onward
        held["carry", tile] = jnp.dot(
            onward * follow_ref[...], spread(middle_ref[:, at]), preferred_element_type=F32
        )

    def finish(part, tile):
        at = source(tile)
        value = held[part, tile] + pack_ref[SKIP : SKIP + 1, at] * gated_ref[span(part), at].astype(F32)
        if part:
            value = value + held["carry", tile]
        local_ref[span(part), target(tile)] = value

    return [
        lambda: carry(0), lambda: inner(0), lambda: carry(1), lambda: inner(1),
        lambda: pick(0, 0), lambda: finish(0, 0), lambda: pick(1, 0), lambda: finish(1, 0),
        lambda: pick(0, 1), lambda: finish(0, 1), lambda: pick(1, 1), lambda: finish(1, 1),
    ]


def local_kernel(
    place_ref, query_ref, halo_ref, gated_ref, pack_ref, taps_ref, middle_ref,
    agree_ref, causal_ref, follow_ref, _,
    local_ref, queries_ref, onward_ref, token_ref,
    mats_a, mats_b, *, side, first,
):
    tokens, channels = local_ref.shape
    token_ref[...] = jnp.zeros_like(token_ref)
    origin = place_ref[side] + first

    def query_jobs(step):
        def one(tile, start):
            at = step * WIDE + tile * LANES
            halo = halo_ref[0, :, lanes_at(origin + at)].astype(F32)
            source = lanes_at(first + at)
            summed = featured(query_ref, source, pack_ref[0:SHORT, source], agree_ref, start, halo)
            queries_ref[start : start + ROWS, lanes_at(at)] = summed.astype(BF16)

        return [
            lambda tile=tile, start=start: one(tile, start)
            for tile in range(2) for start in range(0, tokens, ROWS)
        ]

    def work(step, mats_ref):
        return filter_jobs(
            step, first, gated_ref, pack_ref, middle_ref, mats_ref, causal_ref, follow_ref,
            local_ref, onward_ref,
        )

    chunks = channels // WIDE
    weave(lag_jobs(0, first, taps_ref, mats_a))

    @pl.loop(0, chunks // 2)
    def _(pair):
        step = pair * 2
        weave(work(step, mats_a), lag_jobs(step + 1, first, taps_ref, mats_b), query_jobs(step))
        after = jnp.minimum(step + 2, chunks - 1)
        weave(work(step + 1, mats_b), lag_jobs(after, first, taps_ref, mats_a), query_jobs(step + 1))


def output_kernel(place_ref, enter_ref, *refs, pieces, chunk):
    inputs, (out_ref, held_ref, sems) = refs[:-3], refs[-3:]
    pending = []
    done = 0
    for index, (side, first, count) in enumerate(pieces):
        local_ref, queries_ref, onward_ref = inputs[3 * index : 3 * index + 3]
        carry_ref, rates_ref = inputs[3 * len(pieces) + 2 * side : 3 * len(pieces) + 2 * side + 2]

        def tile(start):
            at, source = lanes_at(start), lanes_at(first + start)
            carry = carry_ref[:, source].astype(F32)
            for part in range(PARTS):
                span = slice(part * PART, (part + 1) * PART)
                if part:
                    carry = carry * jnp.exp(-rates_ref[:, source] * PART)
                carried = jnp.dot(
                    onward_ref[:, at] * enter_ref[span, :], spread(carry), preferred_element_type=F32
                )
                mixed = (local_ref[span, at] + carried).astype(BF16).astype(F32)
                held_ref[span, lanes_at(done + start)] = (
                    queries_ref[span, at].astype(F32) * mixed
                ).astype(BF16)

        for begin in range(0, count, chunk):

            def step(number, carried):
                tile(begin + number * LANES)
                return carried

            lax.fori_loop(0, chunk // LANES, step, 0, unroll=4)
            where = pl.multiple_of(place_ref[side] + (first + begin), chunk)
            copy = pltpu.make_async_copy(
                held_ref.at[:, done + begin : done + begin + chunk],
                out_ref.at[:, pl.ds(where, chunk)],
                sems.at[len(pending)],
            )
            copy.start()
            pending.append(copy)
        done += count
    for copy in pending:
        copy.wait()


def ordered(upper, mine, other):
    mine, other = mine.astype(F32), other.astype(F32)
    return jnp.where(upper, other, mine), jnp.where(upper, mine, other)


def decay(rate, span):
    return jnp.exp(-rate * span)


def weight(flags_ref, index):
    return flags_ref[index : index + 1, 0:1]


def above(flags_ref, index, like):
    row = weight(flags_ref, ROWS_OF_PLACE + index)
    return jnp.broadcast_to(row, like.shape) > 0.5


def pair_kernel(flags_ref, kept_ref, got_ref, rate_ref, first_ref, ends_ref, send_ref, *, tokens):
    first, second = ordered(above(flags_ref, LOW, kept_ref), kept_ref[...], got_ref[...])
    first_ref[...] = first
    ends = second + weight(flags_ref, PAIR_PASS) * decay(rate_ref[...], tokens) * first
    ends_ref[...] = ends
    send_ref[...] = ends.astype(BF16)


def quad_kernel(flags_ref, mine_ref, got_ref, rate_ref, lower_ref, total_ref, send_ref, *, tokens):
    lower, upper = ordered(above(flags_ref, HIGH, mine_ref), mine_ref[...], got_ref[...])
    lower_ref[...] = lower
    total = upper + weight(flags_ref, QUAD_PASS) * decay(rate_ref[...], 2 * tokens) * lower
    total_ref[...] = total
    send_ref[...] = total.astype(BF16)


def round_kernel(flags_ref, total_ref, got_ref, rate_ref, *refs, tokens, number, last):
    rate = rate_ref[...]
    got = got_ref[...].astype(F32)
    at = ROUNDS + 3 * number
    carry = weight(flags_ref, at) * decay(rate, weight(flags_ref, at + 1)) * got
    if number:
        carry, refs = refs[0][...] + carry, refs[1:]
    if not last:
        carry_ref, sum_ref, send_ref = refs
        carry_ref[...] = carry
        before, after = ordered(above(flags_ref, UPSIDES + number, rate), total_ref[...], got)
        total = after + weight(flags_ref, at + 2) * decay(rate, (4 << number) * tokens) * before
        sum_ref[...] = total
        send_ref[...] = total.astype(BF16)
        return
    lower_ref, first_ref, keep_ref, send_ref = refs
    ahead = lower_ref[...] + weight(flags_ref, QUAD_FROM) * decay(rate, 2 * tokens) * carry
    carry = jnp.where(above(flags_ref, HIGH, carry), ahead, carry)
    ahead = first_ref[...] + weight(flags_ref, PAIR_FROM) * decay(rate, tokens) * carry
    keep, send = ordered(above(flags_ref, LOW, carry), carry, ahead)
    keep_ref[...] = keep.astype(BF16)
    send_ref[...] = send.astype(BF16)


def params(mebibytes=20):
    return pltpu.CompilerParams(vmem_limit_bytes=mebibytes * 1024 * 1024)


def cost(flops, size):
    return pl.CostEstimate(flops=flops, bytes_accessed=size, transcendentals=0)


def shaped(shape, dtype):
    return jax.ShapeDtypeStruct(shape, dtype)


def small_call(kernel, name, flags, *operands, outs, tokens_before=(), **static):
    waits = len(tokens_before)
    return pl.pallas_call(
        lambda *refs: kernel(*refs[waits:], **static),
        in_specs=[ANY] * waits + [VMEM] * (1 + len(operands)),
        out_specs=[VMEM] * len(outs),
        out_shape=outs,
        compiler_params=params(),
        cost_estimate=cost(1 << 18, 1 << 18),
        name=name,
    )(*tokens_before, flags, *operands)


def packing(weights, after):
    short, skip, rates, residues = weights
    owned = short.shape[2]
    arrays = (short, skip.reshape(1, owned), rates.T, residues.T)
    arrays = [pltpu.with_memory_space_constraint(array, pltpu.HBM) for array in arrays]
    return pl.pallas_call(
        packing_kernel,
        in_specs=[ANY] + [HBM] * len(arrays),
        out_specs=VMEM,
        out_shape=shaped((PACKED, owned), F32),
        scratch_shapes=[pltpu.VMEM(array.shape, array.dtype) for array in arrays]
        + [pltpu.SemaphoreType.DMA((len(arrays),))],
        compiler_params=params(),
        cost_estimate=cost(1024, 1024),
        name="packing",
    )(after, *arrays)


def placing(segments, streams, owned, devices, fsdp_count):
    tokens = segments.shape[0] // devices
    marks = segments.reshape(-1, LANES)
    outs = [
        shaped((PLACES,), jnp.int32),
        shaped((ROWS_OF_PLACE,), F32),
        shaped((ROWS_OF_PLACE + PLACES, LANES), F32),
        shaped((SHORT - 1, tokens, LANES), F32),
        shaped((PARTS, PART, WIDE), BF16),
        shaped((PART, LANES), BF16),
        shaped((tokens, LANES), BF16),
        shaped((PARTS, LANES, PART), BF16),
        shaped((tokens, owned), BF16),
    ]
    return pl.pallas_call(
        lambda *refs: place_kernel(*refs, devices=devices, tokens=tokens, fsdp_count=fsdp_count),
        in_specs=[HBM, SMEM, HBM],
        out_specs=[SMEM, SMEM] + [VMEM] * (len(outs) - 2),
        out_shape=outs,
        scratch_shapes=[
            pltpu.VMEM(marks.shape, marks.dtype),
            pltpu.SemaphoreType.DMA,
            pltpu.SemaphoreType.DMA((COPIES,)),
        ],
        compiler_params=params(),
        cost_estimate=cost(1024, 1024),
        name="placing",
    )(streams, marks, pltpu.with_memory_space_constraint(marks, pltpu.HBM))


def lags(place, streams, pack, side, name):
    _, tokens, _ = streams.shape
    channels = pack.shape[1]
    outs = [shaped((channels // GROUP, PART), F32), shaped((channels, PART), BF16)]
    operands, specs, scratch = [pack], [VMEM], []
    if side == OWN:
        operands, specs = [place, streams, pack], [SMEM, HBM, VMEM]
        outs.append(shaped((tokens, channels), BF16))
        scratch.append(pltpu.SemaphoreType.DMA((COPIES,)))
    return pl.pallas_call(
        lambda *refs: lag_kernel(*refs, side=side),
        in_specs=specs,
        out_specs=[VMEM] * len(outs),
        out_shape=outs,
        scratch_shapes=scratch,
        compiler_params=params(),
        cost_estimate=cost(1024, 1024),
        name="lags_" + name,
    )(*operands)


def block_states(place, weights, streams, operands, side, passing, name):
    _, tokens, _ = streams.shape
    channels = operands[0].shape[1]
    outs = [
        shaped((tokens, channels), BF16),
        shaped((tokens, channels), BF16),
        shaped((MODES, channels), BF16),
        shaped((MODES, channels), F32),
        shaped((MODES, channels), F32),
    ]
    scratch = [pltpu.SemaphoreType.DMA((COPIES,))]
    if side == OWN:
        outs += [shaped((tokens, channels), BF16)] * 2
        scratch = [pltpu.SemaphoreType.DMA((2 * COPIES,))] + scratch
    return pl.pallas_call(
        lambda *refs: state_kernel(*refs, side=side, passing=passing),
        in_specs=[SMEM, SMEM, HBM] + [VMEM] * len(operands),
        out_specs=[VMEM] * len(outs),
        out_shape=outs,
        scratch_shapes=scratch,
        compiler_params=params(),
        cost_estimate=cost(20 * tokens * channels, 16 * tokens * channels),
        name="block_states_" + name,
    )(place, weights, streams, *operands)


def block_local(place, operands, after, side, first, count, name):
    tokens = operands[0].shape[0]
    return pl.pallas_call(
        lambda *refs: local_kernel(*refs, side=side, first=first),
        in_specs=[SMEM] + [VMEM] * len(operands) + [ANY],
        out_specs=[VMEM] * 4,
        out_shape=[
            shaped((tokens, count), F32),
            shaped((tokens, count), BF16),
            shaped((PART, count), BF16),
            shaped((8, LANES), F32),
        ],
        scratch_shapes=[
            pltpu.VMEM((WIDE // GROUP // 2, PART, WIDE), BF16),
            pltpu.VMEM((WIDE // GROUP // 2, PART, WIDE), BF16),
        ],
        compiler_params=params(),
        cost_estimate=cost(2 * PART * PART * 2 * count * TILE_GROUPS, 40 * tokens * count),
        name="block_local_" + name,
    )(place, *operands, after)


def block_output(place, enter, pieces, locals_, carries, tokens, channels):
    chunk = 512
    return pl.pallas_call(
        lambda *refs: output_kernel(*refs, pieces=pieces, chunk=chunk),
        in_specs=[SMEM] + [VMEM] * (1 + len(locals_) + len(carries)),
        out_specs=HBM,
        out_shape=shaped((tokens, channels), BF16),
        scratch_shapes=[
            pltpu.VMEM((tokens, channels), BF16),
            pltpu.SemaphoreType.DMA((channels // chunk,)),
        ],
        compiler_params=params(),
        cost_estimate=cost(20 * tokens * channels, 8 * tokens * channels),
        name="block_output",
    )(place, enter, *locals_, *carries)


SPAN = 8


def shifted_2(block, axis, distance):
    devices = range(lax.axis_size(axis))
    route = [(i - distance, i) for i in devices if i - distance in devices]
    return lax.ppermute(block, axis, route)


def contract(pattern, left_side, right_side):
    return jnp.einsum(pattern, left_side, right_side, precision=lax.Precision.HIGHEST)


def featurize(block_rows, before_rows, tap_rows, row_marks, before_marks):
    margin = before_rows.shape[1]
    row_count = block_rows.shape[1]
    joined = jnp.concatenate([before_rows, block_rows], axis=1)
    all_marks = jnp.concatenate([before_marks, row_marks])
    summed = block_rows.astype(jnp.float32) * tap_rows[:, 0][:, None, :]
    for offset in range(1, margin + 1):
        shifted = joined[:, margin - offset : margin - offset + row_count].astype(jnp.float32)
        agreeing = all_marks[margin - offset : margin - offset + row_count] == row_marks
        summed = (
            summed
            + jnp.where(agreeing[None, :, None], shifted, 0.0) * tap_rows[:, offset][:, None, :]
        )
    queries = summed[0].astype(jnp.bfloat16)
    gated_prod = (summed[1] * summed[2]).astype(jnp.bfloat16)
    return lax.optimization_barrier((queries, gated_prod))


def tile_filter(gated_prod, tile_marks, decay_rates, mode_gain, rising):
    tile_rows, channels = gated_prod.shape
    groups = channels // GROUP
    block_len = min(128, tile_rows)
    offsets = jnp.arange(block_len, dtype=jnp.float32)
    forward = mode_gain[:, :, None] * jnp.exp(-decay_rates[:, :, None] * offsets)
    backward = jnp.exp(decay_rates[:, :, None] * offsets)
    causal = (offsets[:, None] >= offsets[None, :]).astype(jnp.float32)
    kernel = contract("gmt,gms->gts", forward, backward) * causal
    mode_rates = decay_rates.T[:, :, None]
    closing = jnp.exp(-mode_rates * (block_len - 1.0 - offsets))
    through = jnp.exp(-mode_rates * block_len)
    head_rising = rising[:, :, :block_len]
    values = gated_prod.astype(jnp.float32).reshape(tile_rows, groups, GROUP)
    carried = jnp.zeros((MODES, groups, GROUP), jnp.float32)
    last_seen = jnp.int32(-1)
    pieces = []
    for number in range(tile_rows // block_len):
        block_vals = values[number * block_len : (number + 1) * block_len]
        block_marks = tile_marks[number * block_len : (number + 1) * block_len]
        agreeing = (block_marks[:, None] == block_marks[None, :]).astype(jnp.float32)
        inside = contract("gts,sgc->tgc", kernel * agreeing, block_vals)
        follow = (block_marks == last_seen).astype(jnp.float32)
        inside = inside + follow[:, None, None] * contract("mgt,mgc->tgc", head_rising, carried)
        ending = (block_marks == block_marks[block_len - 1]).astype(jnp.float32)
        fresh_state = contract("mgs,sgc->mgc", closing * ending, block_vals)
        passing = (block_marks[block_len - 1] == last_seen).astype(jnp.float32)
        carried = fresh_state + passing * through * carried
        last_seen = block_marks[block_len - 1]
        pieces.append(inside)
    return (jnp.concatenate(pieces, axis=0), carried)


def narrow_local(streams, segments, short_taps, decay_rates, residues, skip_gain):
    fsdp_count = lax.axis_size("fsdp")
    ctx_count = lax.axis_size("ctx")
    tile_index = lax.axis_index("ctx")
    own_rows = streams.shape[1]
    tile_rows = own_rows * fsdp_count
    margin = SHORT - 1
    padded_marks = jnp.concatenate([jnp.full((margin,), -1, jnp.int32), segments])
    tile_start = tile_index * tile_rows
    tile_marks = lax.dynamic_slice_in_dim(segments, tile_start, tile_rows)
    local_streams = lax.all_to_all(streams, "fsdp", split_axis=2, concat_axis=1, tiled=True)
    before_rows = shifted_2(local_streams[:, tile_rows - margin :, :], "ctx", 1)
    before_marks = lax.dynamic_slice_in_dim(padded_marks, tile_start, margin)
    queries, gated_prod = featurize(
        local_streams, before_rows, short_taps, tile_marks, before_marks
    )
    channels = gated_prod.shape[1]
    groups = channels // GROUP
    mode_gain = residues * jnp.sqrt(-jnp.expm1(-2.0 * decay_rates))
    positions = jnp.arange(tile_rows, dtype=jnp.float32)
    mode_rates = decay_rates.T[:, :, None]
    rising = mode_gain.T[:, :, None] * jnp.exp(-mode_rates * (positions + 1.0))
    local_part, end_state = tile_filter(gated_prod, tile_marks, decay_rates, mode_gain, rising)
    first_mark = tile_marks[0]
    falling = jnp.exp(-mode_rates * (tile_rows - 1.0 - positions))

    def source_state(operand):
        source_vals, source_marks = operand
        chosen = (source_marks == first_mark).astype(jnp.float32)
        return contract(
            "mgs,sgc->mgc",
            falling * chosen,
            source_vals.astype(jnp.float32).reshape(tile_rows, groups, GROUP),
        )

    def empty_state(operand):
        return jnp.zeros((MODES, groups, GROUP), jnp.float32)

    prior_state = jnp.zeros((MODES, groups, GROUP), jnp.float32)
    for distance in range(1, min(SPAN, ctx_count - 1) + 1):
        source_tile = shifted_2(gated_prod, "ctx", distance)
        source_index = tile_index - distance
        source_marks = lax.dynamic_slice_in_dim(
            segments, jnp.maximum(source_index, 0) * tile_rows, tile_rows
        )
        paired = (source_index >= 0) & (source_marks[tile_rows - 1] == first_mark)
        received = lax.cond(paired, source_state, empty_state, (source_tile, source_marks))
        prior_state = prior_state + jnp.exp(-mode_rates * ((distance - 1) * tile_rows)) * received
    prior_mark = first_mark.astype(jnp.float32)
    follow_tile = (tile_marks.astype(jnp.float32) == prior_mark).astype(jnp.float32)
    filtered = local_part + follow_tile[:, None, None] * contract(
        "mgt,mgc->tgc", rising, prior_state
    )
    mixed_out = (
        filtered.reshape(tile_rows, channels) + skip_gain * gated_prod.astype(jnp.float32)
    ).astype(jnp.bfloat16)
    mixed_out = lax.optimization_barrier(mixed_out)
    payload = (queries.astype(jnp.float32) * mixed_out.astype(jnp.float32)).astype(jnp.bfloat16)
    returned = lax.all_to_all(payload, "fsdp", split_axis=0, concat_axis=1, tiled=True)
    return returned


def swap(array, distance, devices):
    route = [(i, i ^ distance) for i in range(devices)]
    return lax.ppermute(array, ("ctx", "fsdp"), route)


def carry_in(flags, sent, kept, rate, devices, tokens, beside):
    wide, lean = shaped(kept.shape, F32), shaped(kept.shape, BF16)

    def call(kernel, name, send, distance, *operands, outs, **static):
        got = swap(send, distance, devices)
        return small_call(
            kernel, name, flags, operands[0], got, rate, *operands[1:], outs=outs, tokens=tokens,
            tokens_before=beside(name, send), **static,
        )

    first, ends, send = call(pair_kernel, "pairs", sent, 1, kept, outs=[wide, wide, lean])
    lower, total, send = call(quad_kernel, "quads", send, 2, ends, outs=[wide, wide, lean])
    carry, number, size = [], 0, 4
    while 2 * size < devices:
        held, total, send = call(
            round_kernel, "round" + str(number), send, size, total, *carry, outs=[wide, wide, lean],
            number=number, last=False,
        )
        carry = [held]
        size, number = 2 * size, number + 1
    keep, send = call(
        round_kernel, "round" + str(number), send, size, total, *carry, lower, first, outs=[lean, lean],
        number=number, last=True,
    )
    beside("end", send)
    return swap(send, 1, devices), keep


def local(streams, segments, short_taps, decay_rates, residues, skip_gain):
    fsdp_count, ctx_count = lax.axis_size("fsdp"), lax.axis_size("ctx")
    devices = fsdp_count * ctx_count
    _, tokens, channels = streams.shape
    if tokens != PARTS * PART or fsdp_count != 2 or devices < 8:
        return narrow_local(streams, segments, short_taps, decay_rates, residues, skip_gain)
    owned = short_taps.shape[2]
    tail = streams[:, tokens - (SHORT - 1) :, :]
    halo = lax.ppermute(tail, ("ctx", "fsdp"), [(i, i + 1) for i in range(devices - 1)])
    streams = pltpu.with_memory_space_constraint(streams, pltpu.HBM)
    own_pack = packing((short_taps, skip_gain, decay_rates, residues), tail)
    place, weights, flags, agree, causal, follow, enter, chosen, keys = placing(
        segments, streams, owned, devices, fsdp_count
    )
    other_pack = lax.ppermute(own_pack, "fsdp", [(0, 1), (1, 0)])
    passing = ROUNDS + 3 * ((devices // 4).bit_length() - 1)
    found = []
    for side, (name, pack) in enumerate((("own", own_pack), ("other", other_pack))):
        taps, fall, *loaded = lags(place, streams, pack, side, name)
        values = loaded[0] if loaded else values
        gated, query, state, middle, spread_rates, *brought = block_states(
            place, weights, streams, (keys, values, halo, pack, fall, agree, chosen), side, passing, name
        )
        if brought:
            keys, values = brought
        operands = (query, halo, gated, pack, taps, middle, agree, causal, follow)
        found.append((operands, state, spread_rates))
    span = owned // 2
    pieces = [(side, first, span) for side in (OWN, OTHER) for first in range(0, owned, span)]
    beside_rounds = {"round0": 1, "round1": 1, "round2": 1}
    waiting, locals_ = list(pieces), []

    def beside(name, array):
        count = len(waiting) if name == "end" else beside_rounds.get(name, 0)
        given = []
        for _ in range(min(count, len(waiting))):
            side, first, size = waiting.pop(0)
            label = "own" if side == OWN else "other"
            *made, token = block_local(
                place, found[side][0], array, side, first, size, label + str(first // size)
            )
            locals_.extend(made)
            given.append(token)
        return given

    carries = carry_in(
        flags, found[0][1], found[1][1], found[1][2], devices, tokens, beside
    )
    sides = [carries[0], found[0][2], carries[1], found[1][2]]
    return block_output(place, enter, pieces, locals_, sides, tokens, channels)


def solution(mesh):
    placed = (
        P(None, ("ctx", "fsdp"), None),
        P(),
        P(None, None, "fsdp"),
        P("fsdp", None),
        P("fsdp", None),
        P("fsdp"),
    )
    return jax.shard_map(
        local, mesh=mesh, in_specs=placed, out_specs=P(("ctx", "fsdp"), None), check_vma=False
    )
```

```python
import jax
import jax.numpy as jnp
from jax import lax
from jax.experimental import pallas as pl
from jax.experimental.pallas import tpu as pltpu
from jax.sharding import PartitionSpec as P

GROUP = 16
MODES = 16
SHORT = 3
LANES = 128
PART = 128
PARTS = 2
WIDE = 256
COPIES = 4
TILES = 16
TILE_GROUPS = LANES // GROUP
ROWS = 64
LOG2E = 1.4426950408889634
F32 = jnp.float32
BF16 = jnp.bfloat16
VMEM = pl.BlockSpec(memory_space=pltpu.VMEM)
SMEM = pl.BlockSpec(memory_space=pltpu.SMEM)
HBM = pl.BlockSpec(memory_space=pltpu.HBM)
ANY = pl.BlockSpec(memory_space=pl.ANY)
SKIP, RATE, GAIN, PACKED = 9, 10, 11, 16
OWN, OTHER, LOW, HIGH, UPSIDES = 0, 1, 2, 3, 4
PAIR_PASS, QUAD_PASS, QUAD_FROM, PAIR_FROM, ROUNDS = 0, 1, 2, 3, 4
ROWS_OF_PLACE, PLACES = 32, 16


def iota(shape, axis):
    return lax.broadcasted_iota(jnp.int32, shape, axis)


def flag(condition):
    return jnp.where(condition, 1.0, 0.0)


def as_column(row):
    return jnp.transpose(jnp.broadcast_to(row, (LANES, row.shape[1])))


def lanes_at(start, size=LANES):
    return pl.ds(pl.multiple_of(start, LANES), size)


def weave(*lists):
    order = sorted(
        ((i + 0.5) / len(jobs), n, i) for n, jobs in enumerate(lists) for i in range(len(jobs))
    )
    for _, n, i in order:
        lists[n][i]()


def featured(x_ref, lanes, taps, agree_ref, start, halo):
    if start == 0:
        here = x_ref[0:ROWS, lanes].astype(F32)
        sub = iota((8, LANES), 0)
        ahead = jnp.where(sub == 6, halo[0:1], jnp.where(sub == 7, halo[1:2], 0.0))
    else:
        both = x_ref[start - 16 : start + ROWS, lanes].astype(F32)
        here, ahead = both[16:], both[8:16]
    joined = jnp.concatenate([ahead, here], axis=0)
    summed = here * taps[0:1]
    for offset in range(1, SHORT):
        shifted = pltpu.roll(joined, offset, 0)[8:]
        agree = agree_ref[offset - 1, start : start + ROWS, :]
        summed = summed + shifted * agree * taps[offset : offset + 1]
    return summed


def spread(state):
    own = iota(state.shape, 1) // GROUP
    return jnp.concatenate(
        [jnp.where(own == group, state, 0.0) for group in range(TILE_GROUPS)], axis=0
    ).astype(BF16)


def diagonal(full):
    own = iota((MODES, LANES), 1) // GROUP
    state = full[:MODES]
    for group in range(1, TILE_GROUPS):
        state = jnp.where(own == group, full[group * MODES : (group + 1) * MODES], state)
    return state


def packing_kernel(*refs):
    sources, x_ref, pack_ref, tail_ref, held, ends_ref, sems = refs[:4], *refs[4:7], refs[7:11], *refs[11:]
    short_ref, skip_ref, rates_ref, residues_ref = held
    last = x_ref.shape[1] - ends_ref.shape[1]
    tail = pltpu.make_async_copy(x_ref.at[:, pl.ds(last, ends_ref.shape[1]), :], ends_ref, sems.at[4])
    tail.start()
    copies = [
        pltpu.make_async_copy(source, target, sems.at[number])
        for number, (source, target) in enumerate(zip(sources, held))
    ]
    for copy in copies:
        copy.start()
    for copy in copies:
        copy.wait()
    for stream in range(3):
        pack_ref[stream * SHORT : (stream + 1) * SHORT, :] = short_ref[stream]
    pack_ref[SKIP : SKIP + 1, :] = skip_ref[...]
    pack_ref[GAIN + 1 :, :] = jnp.zeros((PACKED - GAIN - 1, pack_ref.shape[1]), F32)
    shape = (MODES, LANES)
    own = iota(shape, 1) % MODES == iota(shape, 0)

    def tile(number, carried):
        at = lanes_at(number * LANES)
        first = number * TILE_GROUPS
        source = lanes_at(first // LANES * LANES)
        index = first % LANES + iota(shape, 1) // MODES
        rate = jnp.take_along_axis(rates_ref[:, source], index, axis=1)
        factor = jnp.take_along_axis(residues_ref[:, source], index, axis=1)
        rate = jnp.sum(jnp.where(own, rate, 0.0), axis=0, keepdims=True)
        factor = jnp.sum(jnp.where(own, factor, 0.0), axis=0, keepdims=True)
        half = jnp.tanh(rate)
        pack_ref[RATE : RATE + 1, at] = rate
        pack_ref[GAIN : GAIN + 1, at] = factor * jnp.sqrt(2.0 * half / (1.0 + half))
        return carried

    lax.fori_loop(0, pack_ref.shape[1] // LANES, tile, 0, unroll=8)
    tail.wait()
    for stream in range(3):
        tail_ref[stream] = ends_ref[stream, ends_ref.shape[1] - (SHORT - 1) :, :]


def place_kernel(
    x_ref, spots_ref, marks_ref,
    place_ref, weights_ref, rows_ref, agree_ref, causal_ref, follow_ref, enter_ref, chosen_ref, keys_ref,
    held_ref, sem, moves, *, devices, tokens, fsdp_count,
):
    copy = pltpu.make_async_copy(marks_ref, held_ref, sem)
    copy.start()
    owned = keys_ref.shape[1]
    lines = tokens // LANES
    fsdp_index = lax.axis_index("fsdp")
    block = lax.axis_index("ctx") * fsdp_count + fsdp_index
    brought = start_copies(x_ref, fsdp_index * owned, ((1, keys_ref),), moves)
    place_ref[OWN] = fsdp_index * owned
    place_ref[OTHER] = (1 - fsdp_index) * owned
    place_ref[LOW] = lax.rem(block, 2)
    place_ref[HIGH] = lax.rem(lax.div(block, 2), 2)
    pair = block - lax.rem(block, 2)
    quad = block - lax.rem(block, 4)

    def end_of(index):
        return spots_ref[jnp.maximum(index, 0) * lines + lines - 1, LANES - 1]

    def passes(earlier, later):
        return jnp.where(end_of(earlier) == end_of(later), 1.0, 0.0)

    weights_ref[PAIR_PASS] = passes(pair, pair + 1)
    weights_ref[QUAD_PASS] = passes(quad + 1, quad + 3)
    weights_ref[QUAD_FROM] = passes(quad - 1, quad + 1)
    weights_ref[PAIR_FROM] = passes(pair - 1, pair)
    size, number = 4, 0
    while size < devices:
        start = block - lax.rem(block, 2 * size)
        upside = lax.rem(lax.div(block, size), 2)
        middle = start + size - 1
        place_ref[UPSIDES + number] = upside
        at = ROUNDS + 3 * number
        weights_ref[at] = jnp.where(upside == 1, passes(middle, quad - 1), 0.0)
        weights_ref[at + 1] = (jnp.maximum(quad - 1 - middle, 0) * tokens).astype(F32)
        weights_ref[at + 2] = passes(middle, middle + size)
        size, number = 2 * size, number + 1

    copy.wait()

    def marks_of(index):
        return jnp.concatenate(
            [held_ref[pl.ds(index * lines + line, 1), :] for line in range(lines)], axis=1
        ).astype(F32)

    marks = marks_of(block)
    before = jnp.where(block > 0, marks_of(jnp.maximum(block - 1, 0)), -1.0)
    column = as_column(marks)
    lane = iota(marks.shape, 1)
    for offset in range(1, SHORT):
        row = jnp.where(lane < offset, pltpu.roll(before, offset, 1), pltpu.roll(marks, offset, 1))
        agree_ref[offset - 1] = flag(column == as_column(row))
    for part in range(PARTS):
        span = slice(part * PART, (part + 1) * PART)
        same = column[span] == marks[:, span]
        mask = flag(same & (iota((PART, LANES), 0) >= iota((PART, LANES), 1))).astype(BF16)
        causal_ref[part] = jnp.concatenate([mask] * 2, axis=1)
        last = marks[:, (part + 1) * PART - 1 : (part + 1) * PART]
        chosen_ref[part] = jnp.broadcast_to(flag(marks[:, span] == last), (LANES, PART)).astype(BF16)
    follow_ref[...] = flag(column[PART:] == marks[:, PART - 1 : PART]).astype(BF16)
    enter_ref[...] = flag(column == before[:, tokens - 1 :]).astype(BF16)
    inside = spots_ref[block * lines + PART // LANES - 1, LANES - 1] == end_of(block)
    weights_ref[ROUNDS + 3 * number] = jnp.where(inside, 1.0, 0.0)
    for spare in range(ROUNDS + 3 * number + 1, ROWS_OF_PLACE):
        weights_ref[spare] = 0.0
    for spare in range(UPSIDES + number, PLACES):
        place_ref[spare] = 0
    for number in range(rows_ref.shape[0]):
        value = weights_ref[number] if number < ROWS_OF_PLACE else place_ref[number - ROWS_OF_PLACE].astype(F32)
        rows_ref[number : number + 1, :] = jnp.full((1, LANES), value, F32)
    for copy in brought:
        copy.wait()


def start_copies(x_ref, origin, moves, sems):
    copies = []
    for stream, ref in moves:
        rows = ref.shape[0] // COPIES
        for number in range(COPIES):
            span = slice(number * rows, (number + 1) * rows)
            there = pl.ds(pl.multiple_of(origin, ref.shape[1]), ref.shape[1])
            copies.append(
                pltpu.make_async_copy(x_ref.at[stream, span, there], ref.at[span, :], sems.at[len(copies)])
            )
            copies[-1].start()
    return copies


def lag_kernel(*refs, side):
    copies = []
    if side == OWN:
        place_ref, x_ref, pack_ref, taps_ref, fall_ref, values_ref, sems = refs
        copies = start_copies(x_ref, place_ref[OWN], ((2, values_ref),), sems)
    else:
        pack_ref, taps_ref, fall_ref = refs
    left = (PART - 1 - iota((LANES, PART), 1)).astype(F32)

    def tile(number, carried):
        at = lanes_at(number * LANES)
        fall = jnp.exp2(as_column(pack_ref[RATE : RATE + 1, at] * -LOG2E) * left)
        fall_ref[pl.ds(pl.multiple_of(number * LANES, LANES), LANES), :] = fall.astype(BF16)
        terms = (as_column(pack_ref[GAIN : GAIN + 1, at]) * fall).reshape(TILE_GROUPS, MODES, PART)
        groups = pl.ds(pl.multiple_of(number * TILE_GROUPS, TILE_GROUPS), TILE_GROUPS)
        taps_ref[groups, :] = jnp.sum(terms, axis=1)
        return carried

    lax.fori_loop(0, pack_ref.shape[1] // LANES, tile, 0, unroll=8)
    for copy in copies:
        copy.wait()


def state_kernel(
    place_ref, weights_ref, x_ref, keys_ref, values_ref, halo_ref, pack_ref, fall_ref, agree_ref, chosen_ref,
    gated_ref, query_ref, state_ref, middle_ref, rates_ref, *rest, side, passing,
):
    tokens, channels = gated_ref.shape
    copies = start_copies(x_ref, place_ref[side], ((0, query_ref),), rest[-1])
    if side == OWN:
        copies += start_copies(x_ref, place_ref[OTHER], ((1, rest[0]), (2, rest[1])), rest[2])
    origin = place_ref[side]
    shape = (MODES, LANES)
    index = iota(shape, 1) // GROUP * GROUP + iota(shape, 0)

    def feature_jobs(start, made):
        at = lanes_at(start)

        def one(row):
            halos = [halo_ref[stream, :, lanes_at(origin + start)].astype(F32) for stream in (1, 2)]
            key = featured(keys_ref, at, pack_ref[SHORT : 2 * SHORT, at], agree_ref, row, halos[0])
            value = featured(values_ref, at, pack_ref[2 * SHORT : 3 * SHORT, at], agree_ref, row, halos[1])
            made[row] = (key * value).astype(BF16)
            gated_ref[row : row + ROWS, at] = made[row]

        return [lambda row=row: one(row) for row in range(0, tokens, ROWS)]

    def state_jobs(start, made):
        at = lanes_at(start)
        held = {}

        def product(part):
            fall = fall_ref[pl.ds(pl.multiple_of(start, LANES), LANES), :]
            right = [made[row] for row in range(part * PART, (part + 1) * PART, ROWS)]
            held[part] = jnp.dot(
                fall * chosen_ref[part], jnp.concatenate(right, axis=0), preferred_element_type=F32
            )

        def finish():
            first, last = diagonal(held[0]), diagonal(held[1])
            row = jnp.broadcast_to(pack_ref[RATE : RATE + 1, at], shape)
            rate = jnp.take_along_axis(row, index, axis=1)
            rates_ref[:, at] = rate
            middle_ref[:, at] = first
            onward = jnp.exp(-rate * PART) * weights_ref[passing] * first
            state_ref[:, at] = (last + onward).astype(BF16)

        return [lambda part=part: product(part) for part in range(PARTS)] + [finish]

    @pl.loop(0, channels // (TILES * LANES))
    def _(step):
        made, jobs = {}, []
        for tile in range(TILES):
            start = step * TILES * LANES + tile * LANES
            made = {}
            ahead = feature_jobs(start, made)
            weave(ahead, jobs)
            jobs = state_jobs(start, made)
        weave(jobs)

    for copy in copies:
        copy.wait()


def lag_jobs(step, first, taps_ref, mats_ref):
    held = {}

    def bases(tile):
        at = pl.multiple_of((first + step * WIDE) // GROUP, 8) + tile * TILE_GROUPS
        taps = taps_ref[pl.ds(pl.multiple_of(at, 8), TILE_GROUPS), :]
        index = (iota((8, LANES), 1) + (LANES - 1) - iota((8, LANES), 0)) & (LANES - 1)
        rows = [jnp.broadcast_to(taps[group : group + 1], (8, LANES)) for group in range(TILE_GROUPS)]
        early = [jnp.take_along_axis(row, index, axis=1) for row in rows]
        late = [pltpu.roll(base, 8, 1) for base in early]
        held[tile] = [jnp.concatenate(both, axis=0).astype(BF16) for both in zip(early, late)]

    def rolls(tile, row):
        for group in range(TILE_GROUPS):
            both = held[tile][group]
            odd = group % 2
            mats_ref[tile * 4 + group // 2, row : row + 16, odd * LANES : (odd + 1) * LANES] = (
                pltpu.roll(both, row, 1) if row else both
            )

    jobs = []
    for tile in range(WIDE // LANES):
        jobs.append(lambda tile=tile: bases(tile))
        jobs += [lambda tile=tile, row=row: rolls(tile, row) for row in range(0, PART, 16)]
    return jobs


def filter_jobs(
    step, first, gated_ref, pack_ref, middle_ref, mats_ref, causal_ref, follow_ref,
    local_ref, onward_ref,
):
    held = {}
    odd = iota((16, WIDE), 1) // GROUP % 2
    keep = [jnp.concatenate([flag(odd == i).astype(BF16)] * (PART // 16), axis=0) for i in (0, 1)]
    own = iota((1, LANES), 1) // (2 * GROUP)

    def source(tile):
        return lanes_at(first + step * WIDE + tile * LANES)

    def target(tile):
        return lanes_at(step * WIDE + tile * LANES)

    def span(part):
        return slice(part * PART, (part + 1) * PART)

    def inner(part):
        values = gated_ref[span(part), lanes_at(first + step * WIDE, WIDE)]
        right = jnp.concatenate([values * keep[0], values * keep[1]], axis=0)
        for pair in range(WIDE // GROUP // 2):
            held["full", part, pair] = jnp.dot(
                mats_ref[pair] * causal_ref[part], right, preferred_element_type=F32
            )

    def pick(part, tile):
        value = None
        for i in range(4):
            piece = held["full", part, tile * 4 + i][:, tile * LANES : (tile + 1) * LANES]
            value = piece if value is None else jnp.where(own == i, piece, value)
        held[part, tile] = value

    def carry(tile):
        at = source(tile)
        age = (iota((PART, LANES), 0) + 1).astype(F32)
        rate = pack_ref[RATE : RATE + 1, at] * -LOG2E
        onward = jnp.exp2(rate * age) * pack_ref[GAIN : GAIN + 1, at]
        onward_ref[PART:, target(tile)] = (onward * jnp.exp2(rate * PART)).astype(BF16)
        onward = onward.astype(BF16)
        onward_ref[:PART, target(tile)] = onward
        held["carry", tile] = jnp.dot(
            onward * follow_ref[...], spread(middle_ref[:, at]), preferred_element_type=F32
        )

    def finish(part, tile):
        at = source(tile)
        value = held[part, tile] + pack_ref[SKIP : SKIP + 1, at] * gated_ref[span(part), at].astype(F32)
        if part:
            value = value + held["carry", tile]
        local_ref[span(part), target(tile)] = value

    return [
        lambda: carry(0), lambda: inner(0), lambda: carry(1), lambda: inner(1),
        lambda: pick(0, 0), lambda: finish(0, 0), lambda: pick(1, 0), lambda: finish(1, 0),
        lambda: pick(0, 1), lambda: finish(0, 1), lambda: pick(1, 1), lambda: finish(1, 1),
    ]


def local_kernel(
    place_ref, query_ref, halo_ref, gated_ref, pack_ref, taps_ref, middle_ref,
    agree_ref, causal_ref, follow_ref, _,
    local_ref, queries_ref, onward_ref, token_ref,
    mats_a, mats_b, *, side, first,
):
    tokens, channels = local_ref.shape
    token_ref[...] = jnp.zeros_like(token_ref)
    origin = place_ref[side] + first

    def query_jobs(step):
        def one(tile, start):
            at = step * WIDE + tile * LANES
            halo = halo_ref[0, :, lanes_at(origin + at)].astype(F32)
            source = lanes_at(first + at)
            summed = featured(query_ref, source, pack_ref[0:SHORT, source], agree_ref, start, halo)
            queries_ref[start : start + ROWS, lanes_at(at)] = summed.astype(BF16)

        return [
            lambda tile=tile, start=start: one(tile, start)
            for tile in range(2) for start in range(0, tokens, ROWS)
        ]

    def work(step, mats_ref):
        return filter_jobs(
            step, first, gated_ref, pack_ref, middle_ref, mats_ref, causal_ref, follow_ref,
            local_ref, onward_ref,
        )

    chunks = channels // WIDE
    weave(lag_jobs(0, first, taps_ref, mats_a))

    @pl.loop(0, chunks // 2)
    def _(pair):
        step = pair * 2
        weave(work(step, mats_a), lag_jobs(step + 1, first, taps_ref, mats_b), query_jobs(step))
        after = jnp.minimum(step + 2, chunks - 1)
        weave(work(step + 1, mats_b), lag_jobs(after, first, taps_ref, mats_a), query_jobs(step + 1))


def output_kernel(place_ref, enter_ref, *refs, pieces, chunk):
    inputs, (out_ref, held_ref, sems) = refs[:-3], refs[-3:]
    pending = []
    done = 0
    for index, (side, first, count) in enumerate(pieces):
        local_ref, queries_ref, onward_ref = inputs[3 * index : 3 * index + 3]
        carry_ref = inputs[3 * len(pieces) + side]

        def tile(start):
            at, source = lanes_at(start), lanes_at(first + start)
            carried = jnp.dot(
                onward_ref[:, at] * enter_ref[...],
                spread(carry_ref[:, source].astype(F32)),
                preferred_element_type=F32,
            )
            mixed = (local_ref[:, at] + carried).astype(BF16).astype(F32)
            held_ref[:, lanes_at(done + start)] = (queries_ref[:, at].astype(F32) * mixed).astype(BF16)

        for begin in range(0, count, chunk):

            def step(number, carried):
                tile(begin + number * LANES)
                return carried

            lax.fori_loop(0, chunk // LANES, step, 0, unroll=4)
            where = pl.multiple_of(place_ref[side] + (first + begin), chunk)
            copy = pltpu.make_async_copy(
                held_ref.at[:, done + begin : done + begin + chunk],
                out_ref.at[:, pl.ds(where, chunk)],
                sems.at[len(pending)],
            )
            copy.start()
            pending.append(copy)
        done += count
    for copy in pending:
        copy.wait()


def ordered(upper, mine, other):
    mine, other = mine.astype(F32), other.astype(F32)
    return jnp.where(upper, other, mine), jnp.where(upper, mine, other)


def decay(rate, span):
    return jnp.exp(-rate * span)


def weight(flags_ref, index):
    return flags_ref[index : index + 1, 0:1]


def above(flags_ref, index, like):
    row = weight(flags_ref, ROWS_OF_PLACE + index)
    return jnp.broadcast_to(row, like.shape) > 0.5


def pair_kernel(flags_ref, kept_ref, got_ref, rate_ref, first_ref, ends_ref, send_ref, *, tokens):
    first, second = ordered(above(flags_ref, LOW, kept_ref), kept_ref[...], got_ref[...])
    first_ref[...] = first
    ends = second + weight(flags_ref, PAIR_PASS) * decay(rate_ref[...], tokens) * first
    ends_ref[...] = ends
    send_ref[...] = ends.astype(BF16)


def quad_kernel(flags_ref, mine_ref, got_ref, rate_ref, lower_ref, total_ref, send_ref, *, tokens):
    lower, upper = ordered(above(flags_ref, HIGH, mine_ref), mine_ref[...], got_ref[...])
    lower_ref[...] = lower
    total = upper + weight(flags_ref, QUAD_PASS) * decay(rate_ref[...], 2 * tokens) * lower
    total_ref[...] = total
    send_ref[...] = total.astype(BF16)


def round_kernel(flags_ref, total_ref, got_ref, rate_ref, *refs, tokens, number, last):
    rate = rate_ref[...]
    got = got_ref[...].astype(F32)
    at = ROUNDS + 3 * number
    carry = weight(flags_ref, at) * decay(rate, weight(flags_ref, at + 1)) * got
    if number:
        carry, refs = refs[0][...] + carry, refs[1:]
    if not last:
        carry_ref, sum_ref, send_ref = refs
        carry_ref[...] = carry
        before, after = ordered(above(flags_ref, UPSIDES + number, rate), total_ref[...], got)
        total = after + weight(flags_ref, at + 2) * decay(rate, (4 << number) * tokens) * before
        sum_ref[...] = total
        send_ref[...] = total.astype(BF16)
        return
    lower_ref, first_ref, keep_ref, send_ref = refs
    ahead = lower_ref[...] + weight(flags_ref, QUAD_FROM) * decay(rate, 2 * tokens) * carry
    carry = jnp.where(above(flags_ref, HIGH, carry), ahead, carry)
    ahead = first_ref[...] + weight(flags_ref, PAIR_FROM) * decay(rate, tokens) * carry
    keep, send = ordered(above(flags_ref, LOW, carry), carry, ahead)
    keep_ref[...] = keep.astype(BF16)
    send_ref[...] = send.astype(BF16)


def params(mebibytes=20):
    return pltpu.CompilerParams(vmem_limit_bytes=mebibytes * 1024 * 1024)


def cost(flops, size):
    return pl.CostEstimate(flops=flops, bytes_accessed=size, transcendentals=0)


def shaped(shape, dtype):
    return jax.ShapeDtypeStruct(shape, dtype)


def small_call(kernel, name, flags, *operands, outs, tokens_before=(), **static):
    waits = len(tokens_before)
    return pl.pallas_call(
        lambda *refs: kernel(*refs[waits:], **static),
        in_specs=[ANY] * waits + [VMEM] * (1 + len(operands)),
        out_specs=[VMEM] * len(outs),
        out_shape=outs,
        compiler_params=params(),
        cost_estimate=cost(1 << 18, 1 << 18),
        name=name,
    )(*tokens_before, flags, *operands)


def packing(weights, streams):
    short, skip, rates, residues = weights
    owned, channels = short.shape[2], streams.shape[2]
    arrays = (short, skip.reshape(1, owned), rates.T, residues.T)
    arrays = [pltpu.with_memory_space_constraint(array, pltpu.HBM) for array in arrays]
    return pl.pallas_call(
        packing_kernel,
        in_specs=[HBM] * (len(arrays) + 1),
        out_specs=[VMEM, VMEM],
        out_shape=[shaped((PACKED, owned), F32), shaped((3, SHORT - 1, channels), BF16)],
        scratch_shapes=[pltpu.VMEM(array.shape, array.dtype) for array in arrays]
        + [pltpu.VMEM((3, 16, channels), BF16), pltpu.SemaphoreType.DMA((len(arrays) + 1,))],
        compiler_params=params(),
        cost_estimate=cost(1024, 1024),
        name="packing",
    )(*arrays, streams)


def placing(segments, streams, owned, devices, fsdp_count):
    tokens = segments.shape[0] // devices
    marks = segments.reshape(-1, LANES)
    outs = [
        shaped((PLACES,), jnp.int32),
        shaped((ROWS_OF_PLACE,), F32),
        shaped((ROWS_OF_PLACE + PLACES, LANES), F32),
        shaped((SHORT - 1, tokens, LANES), F32),
        shaped((PARTS, PART, WIDE), BF16),
        shaped((PART, LANES), BF16),
        shaped((tokens, LANES), BF16),
        shaped((PARTS, LANES, PART), BF16),
        shaped((tokens, owned), BF16),
    ]
    return pl.pallas_call(
        lambda *refs: place_kernel(*refs, devices=devices, tokens=tokens, fsdp_count=fsdp_count),
        in_specs=[HBM, SMEM, HBM],
        out_specs=[SMEM, SMEM] + [VMEM] * (len(outs) - 2),
        out_shape=outs,
        scratch_shapes=[
            pltpu.VMEM(marks.shape, marks.dtype),
            pltpu.SemaphoreType.DMA,
            pltpu.SemaphoreType.DMA((COPIES,)),
        ],
        compiler_params=params(),
        cost_estimate=cost(1024, 1024),
        name="placing",
    )(streams, marks, pltpu.with_memory_space_constraint(marks, pltpu.HBM))


def lags(place, streams, pack, side, name):
    _, tokens, _ = streams.shape
    channels = pack.shape[1]
    outs = [shaped((channels // GROUP, PART), F32), shaped((channels, PART), BF16)]
    operands, specs, scratch = [pack], [VMEM], []
    if side == OWN:
        operands, specs = [place, streams, pack], [SMEM, HBM, VMEM]
        outs.append(shaped((tokens, channels), BF16))
        scratch.append(pltpu.SemaphoreType.DMA((COPIES,)))
    return pl.pallas_call(
        lambda *refs: lag_kernel(*refs, side=side),
        in_specs=specs,
        out_specs=[VMEM] * len(outs),
        out_shape=outs,
        scratch_shapes=scratch,
        compiler_params=params(),
        cost_estimate=cost(1024, 1024),
        name="lags_" + name,
    )(*operands)


def block_states(place, weights, streams, operands, side, passing, name):
    _, tokens, _ = streams.shape
    channels = operands[0].shape[1]
    outs = [
        shaped((tokens, channels), BF16),
        shaped((tokens, channels), BF16),
        shaped((MODES, channels), BF16),
        shaped((MODES, channels), F32),
        shaped((MODES, channels), F32),
    ]
    scratch = [pltpu.SemaphoreType.DMA((COPIES,))]
    if side == OWN:
        outs += [shaped((tokens, channels), BF16)] * 2
        scratch = [pltpu.SemaphoreType.DMA((2 * COPIES,))] + scratch
    return pl.pallas_call(
        lambda *refs: state_kernel(*refs, side=side, passing=passing),
        in_specs=[SMEM, SMEM, HBM] + [VMEM] * len(operands),
        out_specs=[VMEM] * len(outs),
        out_shape=outs,
        scratch_shapes=scratch,
        compiler_params=params(),
        cost_estimate=cost(20 * tokens * channels, 16 * tokens * channels),
        name="block_states_" + name,
    )(place, weights, streams, *operands)


def block_local(place, operands, after, side, first, count, name):
    tokens = operands[0].shape[0]
    return pl.pallas_call(
        lambda *refs: local_kernel(*refs, side=side, first=first),
        in_specs=[SMEM] + [VMEM] * len(operands) + [ANY],
        out_specs=[VMEM] * 4,
        out_shape=[
            shaped((tokens, count), F32),
            shaped((tokens, count), BF16),
            shaped((tokens, count), BF16),
            shaped((8, LANES), F32),
        ],
        scratch_shapes=[
            pltpu.VMEM((WIDE // GROUP // 2, PART, WIDE), BF16),
            pltpu.VMEM((WIDE // GROUP // 2, PART, WIDE), BF16),
        ],
        compiler_params=params(),
        cost_estimate=cost(2 * PART * PART * 2 * count * TILE_GROUPS, 40 * tokens * count),
        name="block_local_" + name,
    )(place, *operands, after)


def block_output(place, enter, pieces, locals_, carries, tokens, channels):
    chunk = 512
    return pl.pallas_call(
        lambda *refs: output_kernel(*refs, pieces=pieces, chunk=chunk),
        in_specs=[SMEM] + [VMEM] * (1 + len(locals_) + len(carries)),
        out_specs=HBM,
        out_shape=shaped((tokens, channels), BF16),
        scratch_shapes=[
            pltpu.VMEM((tokens, channels), BF16),
            pltpu.SemaphoreType.DMA((channels // chunk,)),
        ],
        compiler_params=params(),
        cost_estimate=cost(20 * tokens * channels, 8 * tokens * channels),
        name="block_output",
    )(place, enter, *locals_, *carries)


SPAN = 8


def shifted_2(block, axis, distance):
    devices = range(lax.axis_size(axis))
    route = [(i - distance, i) for i in devices if i - distance in devices]
    return lax.ppermute(block, axis, route)


def contract(pattern, left_side, right_side):
    return jnp.einsum(pattern, left_side, right_side, precision=lax.Precision.HIGHEST)


def featurize(block_rows, before_rows, tap_rows, row_marks, before_marks):
    margin = before_rows.shape[1]
    row_count = block_rows.shape[1]
    joined = jnp.concatenate([before_rows, block_rows], axis=1)
    all_marks = jnp.concatenate([before_marks, row_marks])
    summed = block_rows.astype(jnp.float32) * tap_rows[:, 0][:, None, :]
    for offset in range(1, margin + 1):
        shifted = joined[:, margin - offset : margin - offset + row_count].astype(jnp.float32)
        agreeing = all_marks[margin - offset : margin - offset + row_count] == row_marks
        summed = (
            summed
            + jnp.where(agreeing[None, :, None], shifted, 0.0) * tap_rows[:, offset][:, None, :]
        )
    queries = summed[0].astype(jnp.bfloat16)
    gated_prod = (summed[1] * summed[2]).astype(jnp.bfloat16)
    return lax.optimization_barrier((queries, gated_prod))


def tile_filter(gated_prod, tile_marks, decay_rates, mode_gain, rising):
    tile_rows, channels = gated_prod.shape
    groups = channels // GROUP
    block_len = min(128, tile_rows)
    offsets = jnp.arange(block_len, dtype=jnp.float32)
    forward = mode_gain[:, :, None] * jnp.exp(-decay_rates[:, :, None] * offsets)
    backward = jnp.exp(decay_rates[:, :, None] * offsets)
    causal = (offsets[:, None] >= offsets[None, :]).astype(jnp.float32)
    kernel = contract("gmt,gms->gts", forward, backward) * causal
    mode_rates = decay_rates.T[:, :, None]
    closing = jnp.exp(-mode_rates * (block_len - 1.0 - offsets))
    through = jnp.exp(-mode_rates * block_len)
    head_rising = rising[:, :, :block_len]
    values = gated_prod.astype(jnp.float32).reshape(tile_rows, groups, GROUP)
    carried = jnp.zeros((MODES, groups, GROUP), jnp.float32)
    last_seen = jnp.int32(-1)
    pieces = []
    for number in range(tile_rows // block_len):
        block_vals = values[number * block_len : (number + 1) * block_len]
        block_marks = tile_marks[number * block_len : (number + 1) * block_len]
        agreeing = (block_marks[:, None] == block_marks[None, :]).astype(jnp.float32)
        inside = contract("gts,sgc->tgc", kernel * agreeing, block_vals)
        follow = (block_marks == last_seen).astype(jnp.float32)
        inside = inside + follow[:, None, None] * contract("mgt,mgc->tgc", head_rising, carried)
        ending = (block_marks == block_marks[block_len - 1]).astype(jnp.float32)
        fresh_state = contract("mgs,sgc->mgc", closing * ending, block_vals)
        passing = (block_marks[block_len - 1] == last_seen).astype(jnp.float32)
        carried = fresh_state + passing * through * carried
        last_seen = block_marks[block_len - 1]
        pieces.append(inside)
    return (jnp.concatenate(pieces, axis=0), carried)


def narrow_local(streams, segments, short_taps, decay_rates, residues, skip_gain):
    fsdp_count = lax.axis_size("fsdp")
    ctx_count = lax.axis_size("ctx")
    tile_index = lax.axis_index("ctx")
    own_rows = streams.shape[1]
    tile_rows = own_rows * fsdp_count
    margin = SHORT - 1
    padded_marks = jnp.concatenate([jnp.full((margin,), -1, jnp.int32), segments])
    tile_start = tile_index * tile_rows
    tile_marks = lax.dynamic_slice_in_dim(segments, tile_start, tile_rows)
    local_streams = lax.all_to_all(streams, "fsdp", split_axis=2, concat_axis=1, tiled=True)
    before_rows = shifted_2(local_streams[:, tile_rows - margin :, :], "ctx", 1)
    before_marks = lax.dynamic_slice_in_dim(padded_marks, tile_start, margin)
    queries, gated_prod = featurize(
        local_streams, before_rows, short_taps, tile_marks, before_marks
    )
    channels = gated_prod.shape[1]
    groups = channels // GROUP
    mode_gain = residues * jnp.sqrt(-jnp.expm1(-2.0 * decay_rates))
    positions = jnp.arange(tile_rows, dtype=jnp.float32)
    mode_rates = decay_rates.T[:, :, None]
    rising = mode_gain.T[:, :, None] * jnp.exp(-mode_rates * (positions + 1.0))
    local_part, end_state = tile_filter(gated_prod, tile_marks, decay_rates, mode_gain, rising)
    first_mark = tile_marks[0]
    falling = jnp.exp(-mode_rates * (tile_rows - 1.0 - positions))

    def source_state(operand):
        source_vals, source_marks = operand
        chosen = (source_marks == first_mark).astype(jnp.float32)
        return contract(
            "mgs,sgc->mgc",
            falling * chosen,
            source_vals.astype(jnp.float32).reshape(tile_rows, groups, GROUP),
        )

    def empty_state(operand):
        return jnp.zeros((MODES, groups, GROUP), jnp.float32)

    prior_state = jnp.zeros((MODES, groups, GROUP), jnp.float32)
    for distance in range(1, min(SPAN, ctx_count - 1) + 1):
        source_tile = shifted_2(gated_prod, "ctx", distance)
        source_index = tile_index - distance
        source_marks = lax.dynamic_slice_in_dim(
            segments, jnp.maximum(source_index, 0) * tile_rows, tile_rows
        )
        paired = (source_index >= 0) & (source_marks[tile_rows - 1] == first_mark)
        received = lax.cond(paired, source_state, empty_state, (source_tile, source_marks))
        prior_state = prior_state + jnp.exp(-mode_rates * ((distance - 1) * tile_rows)) * received
    prior_mark = first_mark.astype(jnp.float32)
    follow_tile = (tile_marks.astype(jnp.float32) == prior_mark).astype(jnp.float32)
    filtered = local_part + follow_tile[:, None, None] * contract(
        "mgt,mgc->tgc", rising, prior_state
    )
    mixed_out = (
        filtered.reshape(tile_rows, channels) + skip_gain * gated_prod.astype(jnp.float32)
    ).astype(jnp.bfloat16)
    mixed_out = lax.optimization_barrier(mixed_out)
    payload = (queries.astype(jnp.float32) * mixed_out.astype(jnp.float32)).astype(jnp.bfloat16)
    returned = lax.all_to_all(payload, "fsdp", split_axis=0, concat_axis=1, tiled=True)
    return returned


def swap(array, distance, devices):
    route = [(i, i ^ distance) for i in range(devices)]
    return lax.ppermute(array, ("ctx", "fsdp"), route)


def carry_in(flags, sent, kept, rate, devices, tokens, beside):
    wide, lean = shaped(kept.shape, F32), shaped(kept.shape, BF16)

    def call(kernel, name, send, distance, *operands, outs, **static):
        got = swap(send, distance, devices)
        return small_call(
            kernel, name, flags, operands[0], got, rate, *operands[1:], outs=outs, tokens=tokens,
            tokens_before=beside(name, send), **static,
        )

    first, ends, send = call(pair_kernel, "pairs", sent, 1, kept, outs=[wide, wide, lean])
    lower, total, send = call(quad_kernel, "quads", send, 2, ends, outs=[wide, wide, lean])
    carry, number, size = [], 0, 4
    while 2 * size < devices:
        held, total, send = call(
            round_kernel, "round" + str(number), send, size, total, *carry, outs=[wide, wide, lean],
            number=number, last=False,
        )
        carry = [held]
        size, number = 2 * size, number + 1
    keep, send = call(
        round_kernel, "round" + str(number), send, size, total, *carry, lower, first, outs=[lean, lean],
        number=number, last=True,
    )
    beside("end", send)
    return swap(send, 1, devices), keep


def local(streams, segments, short_taps, decay_rates, residues, skip_gain):
    fsdp_count, ctx_count = lax.axis_size("fsdp"), lax.axis_size("ctx")
    devices = fsdp_count * ctx_count
    _, tokens, channels = streams.shape
    if tokens != PARTS * PART or fsdp_count != 2 or devices < 8:
        return narrow_local(streams, segments, short_taps, decay_rates, residues, skip_gain)
    owned = short_taps.shape[2]
    streams = pltpu.with_memory_space_constraint(streams, pltpu.HBM)
    own_pack, tail = packing((short_taps, skip_gain, decay_rates, residues), streams)
    halo = lax.ppermute(tail, ("ctx", "fsdp"), [(i, i + 1) for i in range(devices - 1)])
    place, weights, flags, agree, causal, follow, enter, chosen, keys = placing(
        segments, streams, owned, devices, fsdp_count
    )
    other_pack = lax.ppermute(own_pack, "fsdp", [(0, 1), (1, 0)])
    passing = ROUNDS + 3 * ((devices // 4).bit_length() - 1)
    found = []
    for side, (name, pack) in enumerate((("own", own_pack), ("other", other_pack))):
        taps, fall, *loaded = lags(place, streams, pack, side, name)
        values = loaded[0] if loaded else values
        gated, query, state, middle, spread_rates, *brought = block_states(
            place, weights, streams, (keys, values, halo, pack, fall, agree, chosen), side, passing, name
        )
        if brought:
            keys, values = brought
        operands = (query, halo, gated, pack, taps, middle, agree, causal, follow)
        found.append((operands, state, spread_rates))
    half = owned // 2
    more = half + half // 4
    pieces = [(OWN, 0, half), (OWN, half, half), (OTHER, 0, more), (OTHER, more, owned - more)]
    beside_rounds = {"round0": 1, "round1": 1, "round2": 1}
    waiting, locals_ = list(pieces), []

    def beside(name, array):
        count = len(waiting) if name == "end" else beside_rounds.get(name, 0)
        given = []
        for _ in range(min(count, len(waiting))):
            side, first, size = waiting.pop(0)
            label = "own" if side == OWN else "other"
            *made, token = block_local(
                place, found[side][0], array, side, first, size, label + str(first)
            )
            locals_.extend(made)
            given.append(token)
        return given

    carries = carry_in(
        flags, found[0][1], found[1][1], found[1][2], devices, tokens, beside
    )
    return block_output(place, enter, pieces, locals_, carries, tokens, channels)


def solution(mesh):
    placed = (
        P(None, ("ctx", "fsdp"), None),
        P(),
        P(None, None, "fsdp"),
        P("fsdp", None),
        P("fsdp", None),
        P("fsdp"),
    )
    return jax.shard_map(
        local, mesh=mesh, in_specs=placed, out_specs=P(("ctx", "fsdp"), None), check_vma=False
    )
```

```python
import jax
import jax.numpy as jnp
from jax import lax
from jax.experimental import pallas as pl
from jax.experimental.pallas import tpu as pltpu
from jax.sharding import PartitionSpec as P

GROUP = 16
MODES = 16
SHORT = 3
LANES = 128
PART = 128
PARTS = 2
WIDE = 256
COPIES = 4
TILES = 16
TILE_GROUPS = LANES // GROUP
ROWS = 64
LOG2E = 1.4426950408889634
F32 = jnp.float32
BF16 = jnp.bfloat16
VMEM = pl.BlockSpec(memory_space=pltpu.VMEM)
SMEM = pl.BlockSpec(memory_space=pltpu.SMEM)
HBM = pl.BlockSpec(memory_space=pltpu.HBM)
ANY = pl.BlockSpec(memory_space=pl.ANY)
SKIP, RATE, GAIN, PACKED = 9, 10, 11, 16
OWN, OTHER, LOW, HIGH, UPSIDES = 0, 1, 2, 3, 4
PAIR_PASS, QUAD_PASS, QUAD_FROM, PAIR_FROM, ROUNDS = 0, 1, 2, 3, 4
ROWS_OF_PLACE, PLACES = 32, 16


def iota(shape, axis):
    return lax.broadcasted_iota(jnp.int32, shape, axis)


def flag(condition):
    return jnp.where(condition, 1.0, 0.0)


def as_column(row):
    return jnp.transpose(jnp.broadcast_to(row, (LANES, row.shape[1])))


def lanes_at(start, size=LANES):
    if isinstance(start, int):
        return slice(start, start + size)
    return pl.ds(pl.multiple_of(start, LANES), size)


def weave(*lists):
    order = sorted(
        ((i + 0.5) / len(jobs), n, i) for n, jobs in enumerate(lists) for i in range(len(jobs))
    )
    for _, n, i in order:
        lists[n][i]()


def featured(x_ref, lanes, taps, agree_ref, start, halo):
    if start == 0:
        here = x_ref[0:ROWS, lanes].astype(F32)
        sub = iota((8, LANES), 0)
        ahead = jnp.where(sub == 6, halo[0:1], jnp.where(sub == 7, halo[1:2], 0.0))
    else:
        both = x_ref[start - 16 : start + ROWS, lanes].astype(F32)
        here, ahead = both[16:], both[8:16]
    joined = jnp.concatenate([ahead, here], axis=0)
    summed = here * taps[0:1]
    for offset in range(1, SHORT):
        shifted = pltpu.roll(joined, offset, 0)[8:]
        agree = agree_ref[offset - 1, start : start + ROWS, :]
        summed = summed + shifted * agree * taps[offset : offset + 1]
    return summed


def spread(state):
    own = iota(state.shape, 1) // GROUP
    return jnp.concatenate(
        [jnp.where(own == group, state, 0.0) for group in range(TILE_GROUPS)], axis=0
    ).astype(BF16)


def diagonal(full):
    own = iota((MODES, LANES), 1) // GROUP
    state = full[:MODES]
    for group in range(1, TILE_GROUPS):
        state = jnp.where(own == group, full[group * MODES : (group + 1) * MODES], state)
    return state


def packing_kernel(*refs):
    sources, x_ref, pack_ref, tail_ref, held, ends_ref, sems = refs[:4], *refs[4:7], refs[7:11], *refs[11:]
    short_ref, skip_ref, rates_ref, residues_ref = held
    last = x_ref.shape[1] - ends_ref.shape[1]
    tail = pltpu.make_async_copy(x_ref.at[:, pl.ds(last, ends_ref.shape[1]), :], ends_ref, sems.at[4])
    tail.start()
    copies = [
        pltpu.make_async_copy(source, target, sems.at[number])
        for number, (source, target) in enumerate(zip(sources, held))
    ]
    for copy in copies:
        copy.start()
    for copy in copies:
        copy.wait()
    for stream in range(3):
        pack_ref[stream * SHORT : (stream + 1) * SHORT, :] = short_ref[stream]
    pack_ref[SKIP : SKIP + 1, :] = skip_ref[...]
    pack_ref[GAIN + 1 :, :] = jnp.zeros((PACKED - GAIN - 1, pack_ref.shape[1]), F32)
    shape = (MODES, LANES)
    own = iota(shape, 1) % MODES == iota(shape, 0)

    def tile(number, carried):
        at = lanes_at(number * LANES)
        first = number * TILE_GROUPS
        source = lanes_at(first // LANES * LANES)
        index = first % LANES + iota(shape, 1) // MODES
        rate = jnp.take_along_axis(rates_ref[:, source], index, axis=1)
        factor = jnp.take_along_axis(residues_ref[:, source], index, axis=1)
        rate = jnp.sum(jnp.where(own, rate, 0.0), axis=0, keepdims=True)
        factor = jnp.sum(jnp.where(own, factor, 0.0), axis=0, keepdims=True)
        half = jnp.tanh(rate)
        pack_ref[RATE : RATE + 1, at] = rate
        pack_ref[GAIN : GAIN + 1, at] = factor * jnp.sqrt(2.0 * half / (1.0 + half))
        return carried

    lax.fori_loop(0, pack_ref.shape[1] // LANES, tile, 0, unroll=8)
    tail.wait()
    for stream in range(3):
        tail_ref[stream] = ends_ref[stream, ends_ref.shape[1] - (SHORT - 1) :, :]


def place_kernel(
    x_ref, spots_ref, marks_ref,
    place_ref, weights_ref, rows_ref, agree_ref, causal_ref, follow_ref, enter_ref, chosen_ref, keys_ref,
    held_ref, sem, moves, *, devices, tokens, fsdp_count,
):
    copy = pltpu.make_async_copy(marks_ref, held_ref, sem)
    copy.start()
    owned = keys_ref.shape[1]
    lines = tokens // LANES
    fsdp_index = lax.axis_index("fsdp")
    block = lax.axis_index("ctx") * fsdp_count + fsdp_index
    brought = start_copies(x_ref, fsdp_index * owned, ((1, keys_ref),), moves)
    place_ref[OWN] = fsdp_index * owned
    place_ref[OTHER] = (1 - fsdp_index) * owned
    place_ref[LOW] = lax.rem(block, 2)
    place_ref[HIGH] = lax.rem(lax.div(block, 2), 2)
    pair = block - lax.rem(block, 2)
    quad = block - lax.rem(block, 4)

    def end_of(index):
        return spots_ref[jnp.maximum(index, 0) * lines + lines - 1, LANES - 1]

    def passes(earlier, later):
        return jnp.where(end_of(earlier) == end_of(later), 1.0, 0.0)

    weights_ref[PAIR_PASS] = passes(pair, pair + 1)
    weights_ref[QUAD_PASS] = passes(quad + 1, quad + 3)
    weights_ref[QUAD_FROM] = passes(quad - 1, quad + 1)
    weights_ref[PAIR_FROM] = passes(pair - 1, pair)
    size, number = 4, 0
    while size < devices:
        start = block - lax.rem(block, 2 * size)
        upside = lax.rem(lax.div(block, size), 2)
        middle = start + size - 1
        place_ref[UPSIDES + number] = upside
        at = ROUNDS + 3 * number
        weights_ref[at] = jnp.where(upside == 1, passes(middle, quad - 1), 0.0)
        weights_ref[at + 1] = (jnp.maximum(quad - 1 - middle, 0) * tokens).astype(F32)
        weights_ref[at + 2] = passes(middle, middle + size)
        size, number = 2 * size, number + 1

    copy.wait()

    def marks_of(index):
        return jnp.concatenate(
            [held_ref[pl.ds(index * lines + line, 1), :] for line in range(lines)], axis=1
        ).astype(F32)

    marks = marks_of(block)
    before = jnp.where(block > 0, marks_of(jnp.maximum(block - 1, 0)), -1.0)
    column = as_column(marks)
    lane = iota(marks.shape, 1)
    for offset in range(1, SHORT):
        row = jnp.where(lane < offset, pltpu.roll(before, offset, 1), pltpu.roll(marks, offset, 1))
        agree_ref[offset - 1] = flag(column == as_column(row))
    for part in range(PARTS):
        span = slice(part * PART, (part + 1) * PART)
        same = column[span] == marks[:, span]
        mask = flag(same & (iota((PART, LANES), 0) >= iota((PART, LANES), 1))).astype(BF16)
        causal_ref[part] = jnp.concatenate([mask] * 2, axis=1)
        last = marks[:, (part + 1) * PART - 1 : (part + 1) * PART]
        chosen_ref[part] = jnp.broadcast_to(flag(marks[:, span] == last), (LANES, PART)).astype(BF16)
    follow_ref[...] = flag(column[PART:] == marks[:, PART - 1 : PART]).astype(BF16)
    enter_ref[...] = flag(column == before[:, tokens - 1 :]).astype(BF16)
    inside = spots_ref[block * lines + PART // LANES - 1, LANES - 1] == end_of(block)
    weights_ref[ROUNDS + 3 * number] = jnp.where(inside, 1.0, 0.0)
    for spare in range(ROUNDS + 3 * number + 1, ROWS_OF_PLACE):
        weights_ref[spare] = 0.0
    for spare in range(UPSIDES + number, PLACES):
        place_ref[spare] = 0
    for number in range(rows_ref.shape[0]):
        value = weights_ref[number] if number < ROWS_OF_PLACE else place_ref[number - ROWS_OF_PLACE].astype(F32)
        rows_ref[number : number + 1, :] = jnp.full((1, LANES), value, F32)
    for copy in brought:
        copy.wait()


def start_copies(x_ref, origin, moves, sems):
    copies = []
    for stream, ref in moves:
        rows = ref.shape[0] // COPIES
        for number in range(COPIES):
            span = slice(number * rows, (number + 1) * rows)
            there = pl.ds(pl.multiple_of(origin, ref.shape[1]), ref.shape[1])
            copies.append(
                pltpu.make_async_copy(x_ref.at[stream, span, there], ref.at[span, :], sems.at[len(copies)])
            )
            copies[-1].start()
    return copies


def lag_kernel(*refs, side):
    copies = []
    if side == OWN:
        place_ref, x_ref, pack_ref, taps_ref, fall_ref, values_ref, sems = refs
        copies = start_copies(x_ref, place_ref[OWN], ((2, values_ref),), sems)
    else:
        pack_ref, taps_ref, fall_ref = refs
    left = (PART - 1 - iota((LANES, PART), 1)).astype(F32)

    def tile(number, carried):
        at = lanes_at(number * LANES)
        fall = jnp.exp2(as_column(pack_ref[RATE : RATE + 1, at] * -LOG2E) * left)
        fall_ref[pl.ds(pl.multiple_of(number * LANES, LANES), LANES), :] = fall.astype(BF16)
        terms = (as_column(pack_ref[GAIN : GAIN + 1, at]) * fall).reshape(TILE_GROUPS, MODES, PART)
        groups = pl.ds(pl.multiple_of(number * TILE_GROUPS, TILE_GROUPS), TILE_GROUPS)
        taps_ref[groups, :] = jnp.sum(terms, axis=1)
        return carried

    lax.fori_loop(0, pack_ref.shape[1] // LANES, tile, 0, unroll=8)
    for copy in copies:
        copy.wait()


def state_kernel(
    place_ref, weights_ref, x_ref, keys_ref, values_ref, halo_ref, pack_ref, fall_ref, agree_ref, chosen_ref,
    gated_ref, query_ref, state_ref, middle_ref, rates_ref, *rest, side, passing,
):
    tokens, channels = gated_ref.shape
    copies = start_copies(x_ref, place_ref[side], ((0, query_ref),), rest[-1])
    if side == OWN:
        copies += start_copies(x_ref, place_ref[OTHER], ((1, rest[0]), (2, rest[1])), rest[2])
    origin = place_ref[side]
    shape = (MODES, LANES)
    index = iota(shape, 1) // GROUP * GROUP + iota(shape, 0)

    def feature_jobs(start, made):
        at = lanes_at(start)

        def one(row):
            halos = [halo_ref[stream, :, lanes_at(origin + start)].astype(F32) for stream in (1, 2)]
            key = featured(keys_ref, at, pack_ref[SHORT : 2 * SHORT, at], agree_ref, row, halos[0])
            value = featured(values_ref, at, pack_ref[2 * SHORT : 3 * SHORT, at], agree_ref, row, halos[1])
            made[row] = (key * value).astype(BF16)
            gated_ref[row : row + ROWS, at] = made[row]

        return [lambda row=row: one(row) for row in range(0, tokens, ROWS)]

    def state_jobs(start, made):
        at = lanes_at(start)
        held = {}

        def product(part):
            fall = fall_ref[pl.ds(pl.multiple_of(start, LANES), LANES), :]
            right = [made[row] for row in range(part * PART, (part + 1) * PART, ROWS)]
            held[part] = jnp.dot(
                fall * chosen_ref[part], jnp.concatenate(right, axis=0), preferred_element_type=F32
            )

        def finish():
            first, last = diagonal(held[0]), diagonal(held[1])
            row = jnp.broadcast_to(pack_ref[RATE : RATE + 1, at], shape)
            rate = jnp.take_along_axis(row, index, axis=1)
            rates_ref[:, at] = rate
            middle_ref[:, at] = first
            onward = jnp.exp(-rate * PART) * weights_ref[passing] * first
            state_ref[:, at] = (last + onward).astype(BF16)

        return [lambda part=part: product(part) for part in range(PARTS)] + [finish]

    @pl.loop(0, channels // (TILES * LANES))
    def _(step):
        made, jobs = {}, []
        for tile in range(TILES):
            start = step * TILES * LANES + tile * LANES
            made = {}
            ahead = feature_jobs(start, made)
            weave(ahead, jobs)
            jobs = state_jobs(start, made)
        weave(jobs)

    for copy in copies:
        copy.wait()


def lag_jobs(step, first, taps_ref, mats_ref):
    held = {}

    def bases(tile):
        at = (first + step * WIDE) // GROUP + tile * TILE_GROUPS
        taps = taps_ref[at : at + TILE_GROUPS, :]
        index = (iota((8, LANES), 1) + (LANES - 1) - iota((8, LANES), 0)) & (LANES - 1)
        rows = [jnp.broadcast_to(taps[group : group + 1], (8, LANES)) for group in range(TILE_GROUPS)]
        early = [jnp.take_along_axis(row, index, axis=1) for row in rows]
        late = [pltpu.roll(base, 8, 1) for base in early]
        held[tile] = [jnp.concatenate(both, axis=0).astype(BF16) for both in zip(early, late)]

    def rolls(tile, row):
        for group in range(TILE_GROUPS):
            both = held[tile][group]
            odd = group % 2
            mats_ref[tile * 4 + group // 2, row : row + 16, odd * LANES : (odd + 1) * LANES] = (
                pltpu.roll(both, row, 1) if row else both
            )

    jobs = []
    for tile in range(WIDE // LANES):
        jobs.append(lambda tile=tile: bases(tile))
        jobs += [lambda tile=tile, row=row: rolls(tile, row) for row in range(0, PART, 16)]
    return jobs


def filter_jobs(
    step, first, gated_ref, pack_ref, middle_ref, mats_ref, causal_ref, follow_ref,
    local_ref, onward_ref,
):
    held = {}
    odd = iota((16, WIDE), 1) // GROUP % 2
    keep = [jnp.concatenate([flag(odd == i).astype(BF16)] * (PART // 16), axis=0) for i in (0, 1)]
    own = iota((1, LANES), 1) // (2 * GROUP)

    def source(tile):
        return lanes_at(first + step * WIDE + tile * LANES)

    def target(tile):
        return lanes_at(step * WIDE + tile * LANES)

    def span(part):
        return slice(part * PART, (part + 1) * PART)

    def inner(part):
        values = gated_ref[span(part), lanes_at(first + step * WIDE, WIDE)]
        right = jnp.concatenate([values * keep[0], values * keep[1]], axis=0)
        for pair in range(WIDE // GROUP // 2):
            held["full", part, pair] = jnp.dot(
                mats_ref[pair] * causal_ref[part], right, preferred_element_type=F32
            )

    def pick(part, tile):
        value = None
        for i in range(4):
            piece = held["full", part, tile * 4 + i][:, tile * LANES : (tile + 1) * LANES]
            value = piece if value is None else jnp.where(own == i, piece, value)
        held[part, tile] = value

    def carry(tile):
        at = source(tile)
        age = (iota((PART, LANES), 0) + 1).astype(F32)
        rate = pack_ref[RATE : RATE + 1, at] * -LOG2E
        onward = jnp.exp2(rate * age) * pack_ref[GAIN : GAIN + 1, at]
        onward_ref[PART:, target(tile)] = (onward * jnp.exp2(rate * PART)).astype(BF16)
        onward = onward.astype(BF16)
        onward_ref[:PART, target(tile)] = onward
        held["carry", tile] = jnp.dot(
            onward * follow_ref[...], spread(middle_ref[:, at]), preferred_element_type=F32
        )

    def finish(part, tile):
        at = source(tile)
        value = held[part, tile] + pack_ref[SKIP : SKIP + 1, at] * gated_ref[span(part), at].astype(F32)
        if part:
            value = value + held["carry", tile]
        local_ref[span(part), target(tile)] = value

    return [
        lambda: carry(0), lambda: inner(0), lambda: carry(1), lambda: inner(1),
        lambda: pick(0, 0), lambda: finish(0, 0), lambda: pick(1, 0), lambda: finish(1, 0),
        lambda: pick(0, 1), lambda: finish(0, 1), lambda: pick(1, 1), lambda: finish(1, 1),
    ]


def local_kernel(
    place_ref, query_ref, halo_ref, gated_ref, pack_ref, taps_ref, middle_ref,
    agree_ref, causal_ref, follow_ref, _,
    local_ref, queries_ref, onward_ref, token_ref,
    mats_a, mats_b, *, side, first,
):
    tokens, channels = local_ref.shape
    token_ref[...] = jnp.zeros_like(token_ref)
    origin = place_ref[side] + first

    def query_jobs(step):
        def one(tile, start):
            at = step * WIDE + tile * LANES
            halo = halo_ref[0, :, lanes_at(origin + at)].astype(F32)
            source = lanes_at(first + at)
            summed = featured(query_ref, source, pack_ref[0:SHORT, source], agree_ref, start, halo)
            queries_ref[start : start + ROWS, lanes_at(at)] = summed.astype(BF16)

        return [
            lambda tile=tile, start=start: one(tile, start)
            for tile in range(2) for start in range(0, tokens, ROWS)
        ]

    def work(step, mats_ref):
        return filter_jobs(
            step, first, gated_ref, pack_ref, middle_ref, mats_ref, causal_ref, follow_ref,
            local_ref, onward_ref,
        )

    chunks = channels // WIDE
    weave(lag_jobs(0, first, taps_ref, mats_a))

    buffers = (mats_a, mats_b)
    for step in range(chunks):
        ahead = []
        if step + 1 < chunks:
            ahead = lag_jobs(step + 1, first, taps_ref, buffers[(step + 1) % 2])
        weave(work(step, buffers[step % 2]), ahead, query_jobs(step))


def output_kernel(place_ref, enter_ref, *refs, pieces, chunk):
    inputs, (out_ref, held_ref, sems) = refs[:-3], refs[-3:]
    pending = []
    done = 0
    for index, (side, first, count) in enumerate(pieces):
        local_ref, queries_ref, onward_ref = inputs[3 * index : 3 * index + 3]
        carry_ref = inputs[3 * len(pieces) + side]

        def tile(start):
            at, source = lanes_at(start), lanes_at(first + start)
            carried = jnp.dot(
                onward_ref[:, at] * enter_ref[...],
                spread(carry_ref[:, source].astype(F32)),
                preferred_element_type=F32,
            )
            mixed = (local_ref[:, at] + carried).astype(BF16).astype(F32)
            held_ref[:, lanes_at(done + start)] = (queries_ref[:, at].astype(F32) * mixed).astype(BF16)

        for begin in range(0, count, chunk):

            def step(number, carried):
                tile(begin + number * LANES)
                return carried

            lax.fori_loop(0, chunk // LANES, step, 0, unroll=4)
            where = pl.multiple_of(place_ref[side] + (first + begin), chunk)
            copy = pltpu.make_async_copy(
                held_ref.at[:, done + begin : done + begin + chunk],
                out_ref.at[:, pl.ds(where, chunk)],
                sems.at[len(pending)],
            )
            copy.start()
            pending.append(copy)
        done += count
    for copy in pending:
        copy.wait()


def ordered(upper, mine, other):
    mine, other = mine.astype(F32), other.astype(F32)
    return jnp.where(upper, other, mine), jnp.where(upper, mine, other)


def decay(rate, span):
    return jnp.exp(-rate * span)


def weight(flags_ref, index):
    return flags_ref[index : index + 1, 0:1]


def above(flags_ref, index, like):
    row = weight(flags_ref, ROWS_OF_PLACE + index)
    return jnp.broadcast_to(row, like.shape) > 0.5


def pair_kernel(flags_ref, kept_ref, got_ref, rate_ref, first_ref, ends_ref, send_ref, *, tokens):
    first, second = ordered(above(flags_ref, LOW, kept_ref), kept_ref[...], got_ref[...])
    first_ref[...] = first
    ends = second + weight(flags_ref, PAIR_PASS) * decay(rate_ref[...], tokens) * first
    ends_ref[...] = ends
    send_ref[...] = ends.astype(BF16)


def quad_kernel(flags_ref, mine_ref, got_ref, rate_ref, lower_ref, total_ref, send_ref, *, tokens):
    lower, upper = ordered(above(flags_ref, HIGH, mine_ref), mine_ref[...], got_ref[...])
    lower_ref[...] = lower
    total = upper + weight(flags_ref, QUAD_PASS) * decay(rate_ref[...], 2 * tokens) * lower
    total_ref[...] = total
    send_ref[...] = total.astype(BF16)


def round_kernel(flags_ref, total_ref, got_ref, rate_ref, *refs, tokens, number, last):
    rate = rate_ref[...]
    got = got_ref[...].astype(F32)
    at = ROUNDS + 3 * number
    carry = weight(flags_ref, at) * decay(rate, weight(flags_ref, at + 1)) * got
    if number:
        carry, refs = refs[0][...] + carry, refs[1:]
    if not last:
        carry_ref, sum_ref, send_ref = refs
        carry_ref[...] = carry
        before, after = ordered(above(flags_ref, UPSIDES + number, rate), total_ref[...], got)
        total = after + weight(flags_ref, at + 2) * decay(rate, (4 << number) * tokens) * before
        sum_ref[...] = total
        send_ref[...] = total.astype(BF16)
        return
    lower_ref, first_ref, keep_ref, send_ref = refs
    ahead = lower_ref[...] + weight(flags_ref, QUAD_FROM) * decay(rate, 2 * tokens) * carry
    carry = jnp.where(above(flags_ref, HIGH, carry), ahead, carry)
    ahead = first_ref[...] + weight(flags_ref, PAIR_FROM) * decay(rate, tokens) * carry
    keep, send = ordered(above(flags_ref, LOW, carry), carry, ahead)
    keep_ref[...] = keep.astype(BF16)
    send_ref[...] = send.astype(BF16)


def params(mebibytes=20):
    return pltpu.CompilerParams(vmem_limit_bytes=mebibytes * 1024 * 1024)


def cost(flops, size):
    return pl.CostEstimate(flops=flops, bytes_accessed=size, transcendentals=0)


def shaped(shape, dtype):
    return jax.ShapeDtypeStruct(shape, dtype)


def small_call(kernel, name, flags, *operands, outs, tokens_before=(), **static):
    waits = len(tokens_before)
    return pl.pallas_call(
        lambda *refs: kernel(*refs[waits:], **static),
        in_specs=[ANY] * waits + [VMEM] * (1 + len(operands)),
        out_specs=[VMEM] * len(outs),
        out_shape=outs,
        compiler_params=params(),
        cost_estimate=cost(1 << 18, 1 << 18),
        name=name,
    )(*tokens_before, flags, *operands)


def packing(weights, streams):
    short, skip, rates, residues = weights
    owned, channels = short.shape[2], streams.shape[2]
    arrays = (short, skip.reshape(1, owned), rates.T, residues.T)
    arrays = [pltpu.with_memory_space_constraint(array, pltpu.HBM) for array in arrays]
    return pl.pallas_call(
        packing_kernel,
        in_specs=[HBM] * (len(arrays) + 1),
        out_specs=[VMEM, VMEM],
        out_shape=[shaped((PACKED, owned), F32), shaped((3, SHORT - 1, channels), BF16)],
        scratch_shapes=[pltpu.VMEM(array.shape, array.dtype) for array in arrays]
        + [pltpu.VMEM((3, 16, channels), BF16), pltpu.SemaphoreType.DMA((len(arrays) + 1,))],
        compiler_params=params(),
        cost_estimate=cost(1024, 1024),
        name="packing",
    )(*arrays, streams)


def placing(segments, streams, owned, devices, fsdp_count):
    tokens = segments.shape[0] // devices
    marks = segments.reshape(-1, LANES)
    outs = [
        shaped((PLACES,), jnp.int32),
        shaped((ROWS_OF_PLACE,), F32),
        shaped((ROWS_OF_PLACE + PLACES, LANES), F32),
        shaped((SHORT - 1, tokens, LANES), F32),
        shaped((PARTS, PART, WIDE), BF16),
        shaped((PART, LANES), BF16),
        shaped((tokens, LANES), BF16),
        shaped((PARTS, LANES, PART), BF16),
        shaped((tokens, owned), BF16),
    ]
    return pl.pallas_call(
        lambda *refs: place_kernel(*refs, devices=devices, tokens=tokens, fsdp_count=fsdp_count),
        in_specs=[HBM, SMEM, HBM],
        out_specs=[SMEM, SMEM] + [VMEM] * (len(outs) - 2),
        out_shape=outs,
        scratch_shapes=[
            pltpu.VMEM(marks.shape, marks.dtype),
            pltpu.SemaphoreType.DMA,
            pltpu.SemaphoreType.DMA((COPIES,)),
        ],
        compiler_params=params(),
        cost_estimate=cost(1024, 1024),
        name="placing",
    )(streams, marks, pltpu.with_memory_space_constraint(marks, pltpu.HBM))


def lags(place, streams, pack, side, name):
    _, tokens, _ = streams.shape
    channels = pack.shape[1]
    outs = [shaped((channels // GROUP, PART), F32), shaped((channels, PART), BF16)]
    operands, specs, scratch = [pack], [VMEM], []
    if side == OWN:
        operands, specs = [place, streams, pack], [SMEM, HBM, VMEM]
        outs.append(shaped((tokens, channels), BF16))
        scratch.append(pltpu.SemaphoreType.DMA((COPIES,)))
    return pl.pallas_call(
        lambda *refs: lag_kernel(*refs, side=side),
        in_specs=specs,
        out_specs=[VMEM] * len(outs),
        out_shape=outs,
        scratch_shapes=scratch,
        compiler_params=params(),
        cost_estimate=cost(1024, 1024),
        name="lags_" + name,
    )(*operands)


def block_states(place, weights, streams, operands, side, passing, name):
    _, tokens, _ = streams.shape
    channels = operands[0].shape[1]
    outs = [
        shaped((tokens, channels), BF16),
        shaped((tokens, channels), BF16),
        shaped((MODES, channels), BF16),
        shaped((MODES, channels), F32),
        shaped((MODES, channels), F32),
    ]
    scratch = [pltpu.SemaphoreType.DMA((COPIES,))]
    if side == OWN:
        outs += [shaped((tokens, channels), BF16)] * 2
        scratch = [pltpu.SemaphoreType.DMA((2 * COPIES,))] + scratch
    return pl.pallas_call(
        lambda *refs: state_kernel(*refs, side=side, passing=passing),
        in_specs=[SMEM, SMEM, HBM] + [VMEM] * len(operands),
        out_specs=[VMEM] * len(outs),
        out_shape=outs,
        scratch_shapes=scratch,
        compiler_params=params(),
        cost_estimate=cost(20 * tokens * channels, 16 * tokens * channels),
        name="block_states_" + name,
    )(place, weights, streams, *operands)


def block_local(place, operands, after, side, first, count, name):
    tokens = operands[0].shape[0]
    return pl.pallas_call(
        lambda *refs: local_kernel(*refs, side=side, first=first),
        in_specs=[SMEM] + [VMEM] * len(operands) + [ANY],
        out_specs=[VMEM] * 4,
        out_shape=[
            shaped((tokens, count), F32),
            shaped((tokens, count), BF16),
            shaped((tokens, count), BF16),
            shaped((8, LANES), F32),
        ],
        scratch_shapes=[
            pltpu.VMEM((WIDE // GROUP // 2, PART, WIDE), BF16),
            pltpu.VMEM((WIDE // GROUP // 2, PART, WIDE), BF16),
        ],
        compiler_params=params(),
        cost_estimate=cost(2 * PART * PART * 2 * count * TILE_GROUPS, 40 * tokens * count),
        name="block_local_" + name,
    )(place, *operands, after)


def block_output(place, enter, pieces, locals_, carries, tokens, channels):
    chunk = 512
    return pl.pallas_call(
        lambda *refs: output_kernel(*refs, pieces=pieces, chunk=chunk),
        in_specs=[SMEM] + [VMEM] * (1 + len(locals_) + len(carries)),
        out_specs=HBM,
        out_shape=shaped((tokens, channels), BF16),
        scratch_shapes=[
            pltpu.VMEM((tokens, channels), BF16),
            pltpu.SemaphoreType.DMA((channels // chunk,)),
        ],
        compiler_params=params(),
        cost_estimate=cost(20 * tokens * channels, 8 * tokens * channels),
        name="block_output",
    )(place, enter, *locals_, *carries)


SPAN = 8


def shifted_2(block, axis, distance):
    devices = range(lax.axis_size(axis))
    route = [(i - distance, i) for i in devices if i - distance in devices]
    return lax.ppermute(block, axis, route)


def contract(pattern, left_side, right_side):
    return jnp.einsum(pattern, left_side, right_side, precision=lax.Precision.HIGHEST)


def featurize(block_rows, before_rows, tap_rows, row_marks, before_marks):
    margin = before_rows.shape[1]
    row_count = block_rows.shape[1]
    joined = jnp.concatenate([before_rows, block_rows], axis=1)
    all_marks = jnp.concatenate([before_marks, row_marks])
    summed = block_rows.astype(jnp.float32) * tap_rows[:, 0][:, None, :]
    for offset in range(1, margin + 1):
        shifted = joined[:, margin - offset : margin - offset + row_count].astype(jnp.float32)
        agreeing = all_marks[margin - offset : margin - offset + row_count] == row_marks
        summed = (
            summed
            + jnp.where(agreeing[None, :, None], shifted, 0.0) * tap_rows[:, offset][:, None, :]
        )
    queries = summed[0].astype(jnp.bfloat16)
    gated_prod = (summed[1] * summed[2]).astype(jnp.bfloat16)
    return lax.optimization_barrier((queries, gated_prod))


def tile_filter(gated_prod, tile_marks, decay_rates, mode_gain, rising):
    tile_rows, channels = gated_prod.shape
    groups = channels // GROUP
    block_len = min(128, tile_rows)
    offsets = jnp.arange(block_len, dtype=jnp.float32)
    forward = mode_gain[:, :, None] * jnp.exp(-decay_rates[:, :, None] * offsets)
    backward = jnp.exp(decay_rates[:, :, None] * offsets)
    causal = (offsets[:, None] >= offsets[None, :]).astype(jnp.float32)
    kernel = contract("gmt,gms->gts", forward, backward) * causal
    mode_rates = decay_rates.T[:, :, None]
    closing = jnp.exp(-mode_rates * (block_len - 1.0 - offsets))
    through = jnp.exp(-mode_rates * block_len)
    head_rising = rising[:, :, :block_len]
    values = gated_prod.astype(jnp.float32).reshape(tile_rows, groups, GROUP)
    carried = jnp.zeros((MODES, groups, GROUP), jnp.float32)
    last_seen = jnp.int32(-1)
    pieces = []
    for number in range(tile_rows // block_len):
        block_vals = values[number * block_len : (number + 1) * block_len]
        block_marks = tile_marks[number * block_len : (number + 1) * block_len]
        agreeing = (block_marks[:, None] == block_marks[None, :]).astype(jnp.float32)
        inside = contract("gts,sgc->tgc", kernel * agreeing, block_vals)
        follow = (block_marks == last_seen).astype(jnp.float32)
        inside = inside + follow[:, None, None] * contract("mgt,mgc->tgc", head_rising, carried)
        ending = (block_marks == block_marks[block_len - 1]).astype(jnp.float32)
        fresh_state = contract("mgs,sgc->mgc", closing * ending, block_vals)
        passing = (block_marks[block_len - 1] == last_seen).astype(jnp.float32)
        carried = fresh_state + passing * through * carried
        last_seen = block_marks[block_len - 1]
        pieces.append(inside)
    return (jnp.concatenate(pieces, axis=0), carried)


def narrow_local(streams, segments, short_taps, decay_rates, residues, skip_gain):
    fsdp_count = lax.axis_size("fsdp")
    ctx_count = lax.axis_size("ctx")
    tile_index = lax.axis_index("ctx")
    own_rows = streams.shape[1]
    tile_rows = own_rows * fsdp_count
    margin = SHORT - 1
    padded_marks = jnp.concatenate([jnp.full((margin,), -1, jnp.int32), segments])
    tile_start = tile_index * tile_rows
    tile_marks = lax.dynamic_slice_in_dim(segments, tile_start, tile_rows)
    local_streams = lax.all_to_all(streams, "fsdp", split_axis=2, concat_axis=1, tiled=True)
    before_rows = shifted_2(local_streams[:, tile_rows - margin :, :], "ctx", 1)
    before_marks = lax.dynamic_slice_in_dim(padded_marks, tile_start, margin)
    queries, gated_prod = featurize(
        local_streams, before_rows, short_taps, tile_marks, before_marks
    )
    channels = gated_prod.shape[1]
    groups = channels // GROUP
    mode_gain = residues * jnp.sqrt(-jnp.expm1(-2.0 * decay_rates))
    positions = jnp.arange(tile_rows, dtype=jnp.float32)
    mode_rates = decay_rates.T[:, :, None]
    rising = mode_gain.T[:, :, None] * jnp.exp(-mode_rates * (positions + 1.0))
    local_part, end_state = tile_filter(gated_prod, tile_marks, decay_rates, mode_gain, rising)
    first_mark = tile_marks[0]
    falling = jnp.exp(-mode_rates * (tile_rows - 1.0 - positions))

    def source_state(operand):
        source_vals, source_marks = operand
        chosen = (source_marks == first_mark).astype(jnp.float32)
        return contract(
            "mgs,sgc->mgc",
            falling * chosen,
            source_vals.astype(jnp.float32).reshape(tile_rows, groups, GROUP),
        )

    def empty_state(operand):
        return jnp.zeros((MODES, groups, GROUP), jnp.float32)

    prior_state = jnp.zeros((MODES, groups, GROUP), jnp.float32)
    for distance in range(1, min(SPAN, ctx_count - 1) + 1):
        source_tile = shifted_2(gated_prod, "ctx", distance)
        source_index = tile_index - distance
        source_marks = lax.dynamic_slice_in_dim(
            segments, jnp.maximum(source_index, 0) * tile_rows, tile_rows
        )
        paired = (source_index >= 0) & (source_marks[tile_rows - 1] == first_mark)
        received = lax.cond(paired, source_state, empty_state, (source_tile, source_marks))
        prior_state = prior_state + jnp.exp(-mode_rates * ((distance - 1) * tile_rows)) * received
    prior_mark = first_mark.astype(jnp.float32)
    follow_tile = (tile_marks.astype(jnp.float32) == prior_mark).astype(jnp.float32)
    filtered = local_part + follow_tile[:, None, None] * contract(
        "mgt,mgc->tgc", rising, prior_state
    )
    mixed_out = (
        filtered.reshape(tile_rows, channels) + skip_gain * gated_prod.astype(jnp.float32)
    ).astype(jnp.bfloat16)
    mixed_out = lax.optimization_barrier(mixed_out)
    payload = (queries.astype(jnp.float32) * mixed_out.astype(jnp.float32)).astype(jnp.bfloat16)
    returned = lax.all_to_all(payload, "fsdp", split_axis=0, concat_axis=1, tiled=True)
    return returned


def swap(array, distance, devices):
    route = [(i, i ^ distance) for i in range(devices)]
    return lax.ppermute(array, ("ctx", "fsdp"), route)


def carry_in(flags, sent, kept, rate, devices, tokens, beside):
    wide, lean = shaped(kept.shape, F32), shaped(kept.shape, BF16)

    def call(kernel, name, send, distance, *operands, outs, **static):
        got = swap(send, distance, devices)
        return small_call(
            kernel, name, flags, operands[0], got, rate, *operands[1:], outs=outs, tokens=tokens,
            tokens_before=beside(name, send), **static,
        )

    first, ends, send = call(pair_kernel, "pairs", sent, 1, kept, outs=[wide, wide, lean])
    lower, total, send = call(quad_kernel, "quads", send, 2, ends, outs=[wide, wide, lean])
    carry, number, size = [], 0, 4
    while 2 * size < devices:
        held, total, send = call(
            round_kernel, "round" + str(number), send, size, total, *carry, outs=[wide, wide, lean],
            number=number, last=False,
        )
        carry = [held]
        size, number = 2 * size, number + 1
    keep, send = call(
        round_kernel, "round" + str(number), send, size, total, *carry, lower, first, outs=[lean, lean],
        number=number, last=True,
    )
    beside("end", send)
    return swap(send, 1, devices), keep


def local(streams, segments, short_taps, decay_rates, residues, skip_gain):
    fsdp_count, ctx_count = lax.axis_size("fsdp"), lax.axis_size("ctx")
    devices = fsdp_count * ctx_count
    _, tokens, channels = streams.shape
    if tokens != PARTS * PART or fsdp_count != 2 or devices < 8:
        return narrow_local(streams, segments, short_taps, decay_rates, residues, skip_gain)
    owned = short_taps.shape[2]
    streams = pltpu.with_memory_space_constraint(streams, pltpu.HBM)
    own_pack, tail = packing((short_taps, skip_gain, decay_rates, residues), streams)
    halo = lax.ppermute(tail, ("ctx", "fsdp"), [(i, i + 1) for i in range(devices - 1)])
    place, weights, flags, agree, causal, follow, enter, chosen, keys = placing(
        segments, streams, owned, devices, fsdp_count
    )
    other_pack = lax.ppermute(own_pack, "fsdp", [(0, 1), (1, 0)])
    passing = ROUNDS + 3 * ((devices // 4).bit_length() - 1)
    found = []
    for side, (name, pack) in enumerate((("own", own_pack), ("other", other_pack))):
        taps, fall, *loaded = lags(place, streams, pack, side, name)
        values = loaded[0] if loaded else values
        gated, query, state, middle, spread_rates, *brought = block_states(
            place, weights, streams, (keys, values, halo, pack, fall, agree, chosen), side, passing, name
        )
        if brought:
            keys, values = brought
        operands = (query, halo, gated, pack, taps, middle, agree, causal, follow)
        found.append((operands, state, spread_rates))
    half = owned // 2
    more = half + half // 4
    pieces = [(OWN, 0, half), (OWN, half, half), (OTHER, 0, more), (OTHER, more, owned - more)]
    beside_rounds = {"round0": 1, "round1": 1, "round2": 1}
    waiting, locals_ = list(pieces), []

    def beside(name, array):
        count = len(waiting) if name == "end" else beside_rounds.get(name, 0)
        given = []
        for _ in range(min(count, len(waiting))):
            side, first, size = waiting.pop(0)
            label = "own" if side == OWN else "other"
            *made, token = block_local(
                place, found[side][0], array, side, first, size, label + str(first)
            )
            locals_.extend(made)
            given.append(token)
        return given

    carries = carry_in(
        flags, found[0][1], found[1][1], found[1][2], devices, tokens, beside
    )
    return block_output(place, enter, pieces, locals_, carries, tokens, channels)


def solution(mesh):
    placed = (
        P(None, ("ctx", "fsdp"), None),
        P(),
        P(None, None, "fsdp"),
        P("fsdp", None),
        P("fsdp", None),
        P("fsdp"),
    )
    return jax.shard_map(
        local, mesh=mesh, in_specs=placed, out_specs=P(("ctx", "fsdp"), None), check_vma=False
    )
```
